32 devices in a mesh: seq: 8 (over z, y), section: 4 (over x, core).
Axes of the slice: x: 2, y: 2, z: 4, core: 2. Of those that a mesh axis runs over, the one named last changes fastest.
Arguments:
- block_input: bfloat16 [4, 2048, 512], P('section', 'seq'), may hold values from -8 to 8
- upstream: bfloat16 [4, 2048, 512], P('section', 'seq'), may hold values from -6 to 6
- w_qkv: bfloat16 [4, 512, 768], P('section'), may hold values from -2 to 2
- w_out: bfloat16 [4, 256, 512], P('section'), may hold values from -0.375 to 0.375
- layer_norm_gain: float32 [4, 512], P('section'), may hold values from 0.1 to 1.9
- layer_norm_bias: float32 [4, 512], P('section'), may hold values from -3 to 3
- send_order: int32 [4, 8, 256], P('section', 'seq'), may hold values from 0 to 255, each once within a row
- recv_order: int32 [4, 8, 256], P('section', 'seq'), may hold values from 0 to 255, each once within a row
- patch_lengths: int32 [4, 8, 2], P('section', 'seq'), may hold values from 1 to 224, 256 in all within a row
Outputs:
- handed: bfloat16 [4, 2048, 512], P('section', 'seq')
The draws below stay inside these ranges and needn't reach their ends.
Inputs may be any that keep to these rules, and one draw needn't show every extreme that they name: `send_order`: each device's row is a permutation of 0 to 255. `recv_order`: each device's row is a permutation of 0 to 255. `patch_lengths`: each device's lengths sum to 256; the largest is at most 224.
All inputs are finite; a program needn't handle non-finite values.
Results may differ from the reference program's by a relative error of at most 0.009.
The reference program's roundings to bfloat16 on the way count: a program that leaves them out, or rounds other values in their place, can miss the bound.
Values may be sent and summed in bfloat16 or wider, within the bound.
A program may use at most 64 MiB of HBM per device.

```python
import math
import jax
import jax.numpy as jnp
import numpy as np
from jax import lax

D = 512
HEAD = 16
HEADS = 16
ROWS = 256
PATCHES = 2
HD = 256
BLOCK = 32
PATCH_MOST = 224
TOKENS = 2048
SECTIONS = 4
N_SEQ = 8


def draw_block_input(key, part):
    key = jax.random.fold_in(key, 3)
    noise = jax.random.normal(key, (SECTIONS, TOKENS, D), jnp.float32)
    values = noise
    return jnp.clip(values, -8.0, 8.0).astype(jnp.bfloat16)


def draw_w_qkv(key, part):
    key = jax.random.fold_in(key, 4)
    base = jax.random.normal(key, (SECTIONS, D, 3 * HEADS * HEAD), jnp.float32) / math.sqrt(D)
    return jnp.clip(base, -2.0, 2.0).astype(jnp.bfloat16)


def block_levels(stream_key, extent, shards, low, top_value):
    level, own = 1.0, jax.random.fold_in(stream_key, 6)
    for axis_at, blocks in shards:
        steps = jnp.exp(jax.random.uniform(jax.random.fold_in(own, axis_at), (blocks,), jnp.float32, low / len(shards), top_value / len(shards)))
        level = level * jnp.repeat(steps, extent[axis_at] // blocks).reshape([-1 if axis == axis_at else 1 for axis in range(len(extent))])
    return level


def length_profile(count, total, most, slope):
    portions = [(1 << 20) // math.isqrt(grade ** slope) + 1 for grade in range(2, count + 1)]
    rest, counts = total - most - (count - 1), [1] * (count - 1)
    while rest > 0:
        free = [i for i in range(count - 1) if counts[i] < most]
        whole, left = sum([portions[i] for i in free]), rest
        for i in free:
            addition = min(most - counts[i], max(1, left * portions[i] // whole), rest)
            counts[i] = counts[i] + addition
            rest = rest - addition
    return np.array([most] + counts)


def uneven(rng, count, total, reach, lean):
    if count == 2:
        one = jax.random.randint(rng, (), max(1, total - reach), min(reach, total - 1) + 1)
        return jnp.stack([one, total - one])
    sizes = jnp.asarray(length_profile(count, total, reach, lean), jnp.int32)
    couples = (count - 1) // 2
    giver, receiver = sizes[1:1 + 2 * couples:2], sizes[2:2 + 2 * couples:2]
    slack = jnp.minimum(giver - 1, reach - receiver)
    passed = jax.random.randint(jax.random.fold_in(rng, 1), (couples,), 0, 1 << 20) % (slack + 1)
    sizes = sizes.at[1:1 + 2 * couples:2].set(giver - passed).at[2:2 + 2 * couples:2].set(receiver + passed)
    return sizes[jax.random.permutation(jax.random.fold_in(rng, 2), count)]


def scatter_about(stream_key, extent, deviation, reach, shards=(), kind=jnp.bfloat16):
    values = jax.random.normal(stream_key, extent, jnp.float32) * deviation
    if len(shards) > 0:
        values = block_levels(stream_key, extent, shards, -0.22, 0.18) * values
    return jnp.clip(values, min=-reach, max=reach).astype(kind)


def setup_inputs(seed: int = 0) -> dict:
    seeds = jax.random.split(jax.random.key(seed), 10)
    block_input = draw_block_input(jax.random.fold_in(seeds[9], 71), 0)
    upstream = scatter_about(seeds[1], (SECTIONS, TOKENS, D), 1.0, 6.0, ((0, 4), (1, 8)))
    w_qkv = draw_w_qkv(jax.random.fold_in(seeds[9], 71), 0)
    w_out = scatter_about(seeds[3], (SECTIONS, HD, D), HD ** -0.5, 0.375, ((0, 4),))
    layer_norm_gain = jnp.clip(1.0 + 0.18 * jax.random.normal(seeds[4], (SECTIONS, D), jnp.float32), 0.1, 1.9)
    layer_norm_bias = scatter_about(seeds[5], (SECTIONS, D), 0.5, 3.0, ((0, 4),), jnp.float32)
    send_order = jax.vmap(lambda own: jax.random.permutation(own, ROWS))(jax.random.split(seeds[6], SECTIONS * N_SEQ)).reshape((SECTIONS, N_SEQ, ROWS)).astype(jnp.int32)
    recv_order = jax.vmap(lambda own: jax.random.permutation(own, ROWS))(jax.random.split(seeds[7], SECTIONS * N_SEQ)).reshape((SECTIONS, N_SEQ, ROWS)).astype(jnp.int32)
    patch_lengths = jax.vmap(lambda own: uneven(own, PATCHES, ROWS, PATCH_MOST, 2))(jax.random.split(seeds[8], SECTIONS * N_SEQ)).reshape((SECTIONS, N_SEQ, PATCHES)).astype(jnp.int32)
    return dict(block_input=block_input, upstream=upstream, w_qkv=w_qkv, w_out=w_out, layer_norm_gain=layer_norm_gain, layer_norm_bias=layer_norm_bias, send_order=send_order, recv_order=recv_order, patch_lengths=patch_lengths)


def layer_normalize(rows, gain_weight, shift_bias):
    values = rows.astype(jnp.float32)
    centered_rows = values - lax.optimization_barrier(jnp.mean(values, axis=-1, keepdims=True))
    inverse_deviation = lax.rsqrt(lax.optimization_barrier(jnp.mean(centered_rows * centered_rows, axis=-1, keepdims=True)) + 1e-05)
    standardized_input = centered_rows * inverse_deviation
    normalized_rows = (standardized_input * gain_weight + shift_bias).astype(jnp.bfloat16)
    return (normalized_rows, standardized_input, inverse_deviation)

def layer_norm_backward(normed_gradient, standardized_input, inverse_deviation, gain_weight):
    incoming_gradient = normed_gradient * gain_weight
    gradient_mean = lax.optimization_barrier(jnp.mean(incoming_gradient, axis=-1, keepdims=True))
    cross_term_mean = lax.optimization_barrier(jnp.mean(incoming_gradient * standardized_input, axis=-1, keepdims=True))
    return inverse_deviation * (incoming_gradient - gradient_mean - standardized_input * cross_term_mean)

def attend_grad(qkv, out_grad, lengths):
    count = qkv.shape[0]
    width = out_grad.shape[1]
    heads = width // HEAD
    scale = float(HEAD) ** (-0.5)
    bounds = jnp.cumsum(lengths)
    places = jnp.arange(count, dtype=jnp.int32)
    segment = lax.optimization_barrier(jnp.sum((places[:, None] >= bounds[None, :]).astype(jnp.int32), axis=1))
    same = segment[:, None] == segment[None, :]
    contract_last = (((1,), (1,)), ((), ()))
    contract_first = (((0,), (0,)), ((), ()))

    def one_head(head, grads):
        query = lax.dynamic_slice_in_dim(qkv, head * HEAD, HEAD, 1)
        key_part = lax.dynamic_slice_in_dim(qkv, width + head * HEAD, HEAD, 1)
        value = lax.dynamic_slice_in_dim(qkv, 2 * width + head * HEAD, HEAD, 1)
        dout = lax.dynamic_slice_in_dim(out_grad, head * HEAD, HEAD, 1)
        scores = lax.dot_general(query, key_part, contract_last, preferred_element_type=jnp.float32) * scale
        scores = jnp.where(same, scores, -1e+30)
        top = lax.optimization_barrier(jnp.max(scores, axis=-1, keepdims=True))
        expo = jnp.exp(scores - top)
        probs = expo / lax.optimization_barrier(jnp.sum(expo, axis=-1, keepdims=True))
        weights = probs.astype(jnp.bfloat16)
        dprob = lax.dot_general(dout, value, contract_last, preferred_element_type=jnp.float32)
        inner = lax.optimization_barrier(jnp.sum(dprob * probs, axis=-1, keepdims=True))
        dscore = (scale * probs * (dprob - inner)).astype(jnp.bfloat16)
        dquery = jnp.dot(dscore, key_part, preferred_element_type=jnp.float32).astype(jnp.bfloat16)
        dkey = lax.dot_general(dscore, query, contract_first, preferred_element_type=jnp.float32).astype(jnp.bfloat16)
        dvalue = lax.dot_general(weights, dout, contract_first, preferred_element_type=jnp.float32).astype(jnp.bfloat16)
        grads = lax.dynamic_update_slice_in_dim(grads, dquery, head * HEAD, 1)
        grads = lax.dynamic_update_slice_in_dim(grads, dkey, width + head * HEAD, 1)
        grads = lax.dynamic_update_slice_in_dim(grads, dvalue, 2 * width + head * HEAD, 1)
        return grads
    empty = jnp.zeros((count, 3 * width), jnp.bfloat16)
    return lax.fori_loop(0, heads, one_head, empty)

def reference(block_input, upstream, w_qkv, w_out, layer_norm_gain, layer_norm_bias, send_order, recv_order, patch_lengths):
    totals = []
    contract_last = (((1,), (1,)), ((), ()))
    for section_index in range(1, SECTIONS):
        places = recv_order[section_index]
        source_dev = places // BLOCK
        slot = places % BLOCK
        target = jnp.arange(N_SEQ, dtype=jnp.int32)[:, None]
        position = target * BLOCK + slot
        patch_source = (source_dev * ROWS + send_order[section_index][source_dev, position]).reshape(-1).astype(jnp.int32)
        patch_token_rows = block_input[section_index][patch_source]
        normalized_rows, standardized_input, inverse_deviation = layer_normalize(patch_token_rows, layer_norm_gain[section_index], layer_norm_bias[section_index])
        qkv = jnp.dot(normalized_rows, w_qkv[section_index], preferred_element_type=jnp.float32).astype(jnp.bfloat16)
        out_common = lax.dot_general(upstream[section_index], w_out[section_index], contract_last, preferred_element_type=jnp.float32).astype(jnp.bfloat16)
        out_grad = out_common[patch_source]
        dqkv = lax.map(lambda items: attend_grad(items[0], items[1], items[2]), (qkv.reshape(N_SEQ, ROWS, 3 * HD), out_grad.reshape(N_SEQ, ROWS, HD), patch_lengths[section_index]))
        dqkv = dqkv.reshape(TOKENS, 3 * HD)
        normed_gradient = lax.dot_general(dqkv, w_qkv[section_index], contract_last, preferred_element_type=jnp.float32)
        branch_output = layer_norm_backward(normed_gradient, standardized_input, inverse_deviation, layer_norm_gain[section_index]).astype(jnp.bfloat16)
        common = jnp.zeros((TOKENS, D), jnp.bfloat16).at[patch_source].set(branch_output)
        total = (upstream[section_index].astype(jnp.float32) + common.astype(jnp.float32)).astype(jnp.bfloat16)
        totals.append(total)
    handed = jnp.stack(totals + [jnp.zeros((TOKENS, D), jnp.bfloat16)], axis=0)
    return handed
```

```python
import functools
import math

import jax
import jax.numpy as jnp
from jax import lax
from jax.experimental import pallas as pl
from jax.experimental.pallas import tpu as pltpu
from jax.sharding import PartitionSpec as P

HEAD = 16
MESH = pl.DeviceIdType.MESH
LAST = (((1,), (1,)), ((), ()))
GROUP = 4


def dot(a, b):
    return jnp.dot(a, b, preferred_element_type=jnp.float32)


def dot_nt(a, b):
    return lax.dot_general(a, b, LAST, preferred_element_type=jnp.float32)


def each(first, count, body):
    if count - first <= 8:
        for step in range(first, count):
            body(step)
    else:
        lax.fori_loop(first, count, lambda step, carry: (body(step), carry)[1], 0)


def iota(shape, axis):
    return lax.broadcasted_iota(jnp.int32, shape, axis)


def kernel(
    n,
    sections,
    x_ref,
    up_ref,
    w_ref,
    wo_ref,
    gain_ref,
    bias_ref,
    send_ref,
    recv_ref,
    len_ref,
    out_ref,
    send_x,
    recv_x,
    send_o,
    recv_o,
    send_b,
    recv_b,
    up_next,
    order_own,
    order_next,
    xhat_ref,
    q_ref,
    k_ref,
    v_ref,
    kt_ref,
    do_ref,
    feat_q,
    feat_k,
    dqt_ref,
    dk_ref,
    dv_ref,
    sx_sem,
    rx_sem,
    so_sem,
    ro_sem,
    sb_sem,
    rb_sem,
    up_sem,
    order_sem,
):
    me = lax.axis_index("seq")
    section = lax.axis_index("section")
    rows, wide = x_ref.shape[1], x_ref.shape[2]
    width = wo_ref.shape[1]
    slot = send_x.shape[1]
    block = rows // n
    half = 128

    def spread(values):
        if slot == block:
            return values.reshape(n, slot, values.shape[1])
        place = iota((n * slot, rows), 0)
        source = jnp.where(place % slot < block, place // slot * block + place % slot, -1)
        pick = (source == iota((n * slot, rows), 1)).astype(jnp.bfloat16)
        return dot(pick, values).astype(jnp.bfloat16).reshape(n, slot, values.shape[1])

    def gather(values):
        values = values.reshape(n * slot, values.shape[2])
        if slot == block:
            return values
        place = iota((rows, n * slot), 0)
        pick = (place // block * slot + place % block == iota((rows, n * slot), 1)).astype(jnp.bfloat16)
        return dot(pick, values).astype(jnp.bfloat16)

    def x_copy(local, there, peer):
        return pltpu.make_async_remote_copy(
            send_x.at[local], recv_x.at[there], sx_sem.at[local], rx_sem.at[there],
            device_id=(peer, section), device_id_type=MESH,
        )

    def o_copy(local, there, peer):
        return pltpu.make_async_remote_copy(
            send_o.at[local], recv_o.at[there], so_sem.at[local], ro_sem.at[there],
            device_id=(peer, section), device_id_type=MESH,
        )

    def b_copy(local, there, peer):
        return pltpu.make_async_remote_copy(
            send_b.at[local], recv_b.at[there], sb_sem.at[local], rb_sem.at[there],
            device_id=(peer, section - 1), device_id_type=MESH,
        )

    def up_copy():
        return pltpu.make_async_remote_copy(
            up_ref.at[0], up_next, up_sem.at[0], up_sem.at[1],
            device_id=(me, section - 1), device_id_type=MESH,
        )

    def order_copy():
        return pltpu.make_async_remote_copy(
            order_own, order_next, order_sem.at[0], order_sem.at[1],
            device_id=(me, section - 1), device_id_type=MESH,
        )

    barrier = pltpu.get_barrier_semaphore()

    @pl.when(section > 0)
    def _():
        def greet(step):
            pl.semaphore_signal(
                barrier, inc=1, device_id=(lax.rem(me + step, n), section), device_id_type=MESH
            )

        each(1, n, greet)

    @pl.when(section < sections - 1)
    def _():
        def greet(step):
            pl.semaphore_signal(
                barrier, inc=1, device_id=(lax.rem(me + step, n), section + 1), device_id_type=MESH
            )

        each(0, n, greet)

    @pl.when(section > 0)
    def _():
        order_own[...] = jnp.broadcast_to(send_ref[0], order_own.shape)
        row_of = send_ref[0].astype(jnp.float32)
        eye = iota((rows, rows), 0) == iota((rows, rows), 1)
        column = jnp.sum(jnp.where(eye, row_of, 0.0), axis=1, keepdims=True).astype(jnp.int32)
        pick = jnp.where(column == iota((rows, rows), 1), 1.0, 0.0).astype(jnp.bfloat16)
        send_x[...] = spread(dot(pick, x_ref[0]).astype(jnp.bfloat16))
        pl.semaphore_wait(barrier, 2 * n - 1)
        each(1, n, lambda step: x_copy(lax.rem(me + step, n), me, lax.rem(me + step, n)).start())
        out_common = dot_nt(up_ref[0], wo_ref[0]).astype(jnp.bfloat16)
        send_o[...] = spread(dot(pick, out_common).astype(jnp.bfloat16))
        each(1, n, lambda step: o_copy(lax.rem(me + step, n), me, lax.rem(me + step, n)).start())
        up_copy().start()
        order_copy().start()
        recv_x[me] = send_x[me]
        recv_o[me] = send_o[me]

        place = iota((1, rows), 1)
        end = jnp.int32(0)
        segment = jnp.zeros((1, rows), jnp.float32)
        for patch in range(len_ref.shape[2]):
            end = end + len_ref[0, 0, patch]
            segment = segment + jnp.where(place >= end, 1.0, 0.0)
        at = recv_ref[0] == iota((rows, rows), 0)
        patch_of = jnp.sum(jnp.where(at, segment, 0.0), axis=1, keepdims=True).astype(jnp.int32)
        lanes = iota((rows, half), 1)
        feat_k[...] = jnp.where(patch_of == lanes, 1.0, 0.0).astype(jnp.bfloat16)
        feat_q[...] = jnp.where(patch_of == lanes, 0.0, -1e30).astype(jnp.bfloat16)

        def x_wait(step):
            peer = lax.rem(me + step, n)
            x_copy(peer, peer, peer).wait_recv()

        each(1, n, x_wait)
        values = gather(recv_x[...]).astype(jnp.float32)
        centered = values - jnp.mean(values, axis=-1, keepdims=True)
        inverse = lax.rsqrt(jnp.mean(centered * centered, axis=-1, keepdims=True) + 1e-05)
        xhat = centered * inverse
        xhat_ref[...] = xhat
        normed = (xhat * gain_ref[...] + bias_ref[...]).astype(jnp.bfloat16)
        q_ref[...] = dot(normed, w_ref[0, :, :width]).astype(jnp.bfloat16)
        key = dot(normed, w_ref[0, :, width : 2 * width]).astype(jnp.bfloat16)
        k_ref[...] = key
        kt_ref[...] = key.astype(jnp.float32).T.astype(jnp.bfloat16)
        v_ref[...] = dot(normed, w_ref[0, :, 2 * width :]).astype(jnp.bfloat16)

        def o_wait(step):
            peer = lax.rem(me + step, n)
            o_copy(peer, peer, peer).wait_recv()

        each(1, n, o_wait)
        do_ref[...] = gather(recv_o[...])

        rate = float(HEAD) ** (-0.5) * math.log2(math.e)
        lane_head = iota((rows, half), 1) // HEAD
        zero = jnp.zeros((rows, half), jnp.bfloat16)
        for part in range(width // half):
            columns = slice(part * half, (part + 1) * half)

            def some_heads(group, carry, columns=columns, part=part):
                query, key, value, dout = q_ref[:, columns], k_ref[:, columns], v_ref[:, columns], do_ref[:, columns]
                query_right = jnp.concatenate([query, feat_q[...]], axis=1)
                mine = [lane_head == group * GROUP + i for i in range(GROUP)]
                keys = jnp.concatenate(
                    [jnp.concatenate([jnp.where(m, key, zero), feat_k[...]], axis=1) for m in mine], axis=0
                )
                values = jnp.concatenate([jnp.where(m, value, zero) for m in mine], axis=0)
                scores = dot_nt(keys, query_right)
                dprobs = dot_nt(values, dout)
                weights, dscores = [], []
                for i in range(GROUP):
                    score = scores[i * rows : (i + 1) * rows]
                    dprob = dprobs[i * rows : (i + 1) * rows]
                    expo = jnp.exp2((score - jnp.max(score, axis=0, keepdims=True)) * rate)
                    probs = expo * (1.0 / jnp.sum(expo, axis=0, keepdims=True))
                    inner = jnp.sum(dprob * probs, axis=0, keepdims=True)
                    weights.append(probs.astype(jnp.bfloat16))
                    dscores.append((probs * (dprob - inner)).astype(jnp.bfloat16))
                dkeys = dot(jnp.concatenate(dscores, axis=0), query)
                dvalues = dot(jnp.concatenate(weights, axis=0), dout)
                dkey, dvalue = dk_ref[:, columns], dv_ref[:, columns]
                for i in range(GROUP):
                    dkey = jnp.where(mine[i], dkeys[i * rows : (i + 1) * rows], dkey)
                    dvalue = jnp.where(mine[i], dvalues[i * rows : (i + 1) * rows], dvalue)
                    start = pl.multiple_of(part * half + (group * GROUP + i) * HEAD, HEAD)
                    dqt_ref[pl.ds(start, HEAD), :] = dot(kt_ref[pl.ds(start, HEAD), :], dscores[i])
                dk_ref[:, columns] = dkey
                dv_ref[:, columns] = dvalue
                return carry

            lax.fori_loop(0, half // HEAD // GROUP, some_heads, 0)

        scale = float(HEAD) ** (-0.5)
        dquery = (dqt_ref[...].T * scale).astype(jnp.bfloat16)
        dkey = (dk_ref[...] * scale).astype(jnp.bfloat16)
        dqkv = jnp.concatenate([dquery, dkey, dv_ref[...].astype(jnp.bfloat16)], axis=1)
        grad = dot_nt(dqkv, w_ref[0]) * gain_ref[...]
        xhat = xhat_ref[...]
        mean = jnp.mean(grad, axis=-1, keepdims=True)
        cross = jnp.mean(grad * xhat, axis=-1, keepdims=True)
        branch = inverse * (grad - mean - xhat * cross)
        send_b[...] = spread(branch.astype(jnp.bfloat16))
        each(0, n, lambda step: b_copy(lax.rem(me + step, n), me, lax.rem(me + step, n)).start())

    @pl.when(section < sections - 1)
    def _():
        order_copy().wait_recv()
        up_copy().wait_recv()
        pick = jnp.where(order_next[0:1, :] == iota((rows, rows), 0), 1.0, 0.0).astype(jnp.bfloat16)

        def b_wait(step):
            peer = lax.rem(me + step, n)
            b_copy(peer, peer, peer).wait_recv()

        each(0, n, b_wait)
        branch = dot(pick, gather(recv_b[...]))
        out_ref[0] = (up_next[...].astype(jnp.float32) + branch).astype(jnp.bfloat16)

    @pl.when(section == sections - 1)
    def _():
        out_ref[...] = jnp.zeros_like(out_ref)

    @pl.when(section > 0)
    def _():
        def sent(step):
            peer = lax.rem(me + step, n)
            x_copy(peer, me, peer).wait_send()
            o_copy(peer, me, peer).wait_send()

        each(1, n, sent)

        def sent_back(step):
            peer = lax.rem(me + step, n)
            b_copy(peer, me, peer).wait_send()

        each(0, n, sent_back)
        up_copy().wait_send()
        order_copy().wait_send()


def per_device(x, up, w_qkv, w_out, gain, bias, send_order, recv_order, lengths):
    n, sections = lax.axis_size("seq"), lax.axis_size("section")
    rows, wide = x.shape[1], x.shape[2]
    width = w_out.shape[1]
    slot = max(rows // n, 16)
    vmem = pl.BlockSpec(memory_space=pltpu.VMEM)
    smem = pl.BlockSpec(memory_space=pltpu.SMEM)
    bf16, f32 = jnp.bfloat16, jnp.float32
    dma = pltpu.SemaphoreType.DMA
    return pl.pallas_call(
        functools.partial(kernel, n, sections),
        out_shape=jax.ShapeDtypeStruct(x.shape, bf16),
        in_specs=[vmem] * 8 + [smem],
        out_specs=vmem,
        scratch_shapes=[
            pltpu.VMEM((n, slot, wide), bf16),
            pltpu.VMEM((n, slot, wide), bf16),
            pltpu.VMEM((n, slot, width), bf16),
            pltpu.VMEM((n, slot, width), bf16),
            pltpu.VMEM((n, slot, wide), bf16),
            pltpu.VMEM((n, slot, wide), bf16),
            pltpu.VMEM((rows, wide), bf16),
            pltpu.VMEM((8, rows), jnp.int32),
            pltpu.VMEM((8, rows), jnp.int32),
            pltpu.VMEM((rows, wide), f32),
            pltpu.VMEM((rows, width), bf16),
            pltpu.VMEM((rows, width), bf16),
            pltpu.VMEM((rows, width), bf16),
            pltpu.VMEM((width, rows), bf16),
            pltpu.VMEM((rows, width), bf16),
            pltpu.VMEM((rows, 128), bf16),
            pltpu.VMEM((rows, 128), bf16),
            pltpu.VMEM((width, rows), f32),
            pltpu.VMEM((rows, width), f32),
            pltpu.VMEM((rows, width), f32),
            dma((n,)),
            dma((n,)),
            dma((n,)),
            dma((n,)),
            dma((n,)),
            dma((n,)),
            dma((2,)),
            dma((2,)),
        ],
        compiler_params=pltpu.CompilerParams(
            collective_id=0, has_side_effects=True, vmem_limit_bytes=40 * 1024 * 1024
        ),
        name="patch_attention_grad",
    )(x, up, w_qkv, w_out, gain, bias, send_order, recv_order, lengths)


def solution(mesh):
    return jax.shard_map(
        per_device,
        mesh=mesh,
        in_specs=(
            P("section", "seq", None),
            P("section", "seq", None),
            P("section", None, None),
            P("section", None, None),
            P("section", None),
            P("section", None),
            P("section", "seq", None),
            P("section", "seq", None),
            P("section", "seq", None),
        ),
        out_specs=P("section", "seq", None),
        check_vma=False,
    )
```

```python
import functools
import math

import jax
import jax.numpy as jnp
from jax import lax
from jax.experimental import pallas as pl
from jax.experimental.pallas import tpu as pltpu
from jax.sharding import PartitionSpec as P

HEAD = 16
MESH = pl.DeviceIdType.MESH
LAST = (((1,), (1,)), ((), ()))
GROUP = 4


def dot(a, b):
    return jnp.dot(a, b, preferred_element_type=jnp.float32)


def dot_nt(a, b):
    return lax.dot_general(a, b, LAST, preferred_element_type=jnp.float32)


def each(first, count, body):
    if count - first <= 8:
        for step in by_distance(first, count):
            body(step)
    else:
        lax.fori_loop(first, count, lambda step, carry: (body(step), carry)[1], 0)


def by_distance(first, count):
    return sorted(range(first, count), key=lambda step: (abs(step - count // 2), step))


def iota(shape, axis):
    return lax.broadcasted_iota(jnp.int32, shape, axis)


def kernel(
    n,
    sections,
    x_hbm,
    up_hbm,
    w_hbm,
    wo_hbm,
    gain_hbm,
    bias_hbm,
    send_hbm,
    recv_hbm,
    len_hbm,
    out_ref,
    x_ref,
    up_ref,
    w_ref,
    wo_ref,
    gain_ref,
    bias_ref,
    send_ref,
    recv_ref,
    len_ref,
    load_sem,
    send_x,
    recv_x,
    send_o,
    recv_o,
    send_b,
    recv_b,
    up_next,
    order_own,
    order_next,
    xhat_ref,
    q_ref,
    k_ref,
    v_ref,
    kt_ref,
    do_ref,
    feat_q,
    feat_k,
    dqt_ref,
    probs_ref,
    dqkv_ref,
    inverse_ref,
    dk_ref,
    dv_ref,
    sx_sem,
    rx_sem,
    so_sem,
    ro_sem,
    sb_sem,
    rb_sem,
    up_sem,
    order_sem,
):
    me = lax.axis_index("seq")
    section = lax.axis_index("section")
    rows, wide = x_ref.shape[1], x_ref.shape[2]
    width = wo_ref.shape[1]
    slot = send_x.shape[1]
    block = rows // n
    half = 128

    def spread(values):
        if slot == block:
            return values.reshape(n, slot, values.shape[1])
        place = iota((n * slot, rows), 0)
        source = jnp.where(place % slot < block, place // slot * block + place % slot, -1)
        pick = (source == iota((n * slot, rows), 1)).astype(jnp.bfloat16)
        return dot(pick, values).astype(jnp.bfloat16).reshape(n, slot, values.shape[1])

    def gather(values):
        values = values.reshape(n * slot, values.shape[2])
        if slot == block:
            return values
        place = iota((rows, n * slot), 0)
        pick = (place // block * slot + place % block == iota((rows, n * slot), 1)).astype(jnp.bfloat16)
        return dot(pick, values).astype(jnp.bfloat16)

    def x_copy(local, there, peer):
        return pltpu.make_async_remote_copy(
            send_x.at[local], recv_x.at[there], sx_sem.at[local], rx_sem.at[there],
            device_id=(peer, section), device_id_type=MESH,
        )

    def o_copy(local, there, peer):
        return pltpu.make_async_remote_copy(
            send_o.at[local], recv_o.at[there], so_sem.at[local], ro_sem.at[there],
            device_id=(peer, section), device_id_type=MESH,
        )

    def b_copy(local, there, peer):
        return pltpu.make_async_remote_copy(
            send_b.at[local], recv_b.at[there], sb_sem.at[local], rb_sem.at[there],
            device_id=(peer, section - 1), device_id_type=MESH,
        )

    def up_copy():
        return pltpu.make_async_remote_copy(
            up_ref.at[0], up_next, up_sem.at[0], up_sem.at[1],
            device_id=(me, section - 1), device_id_type=MESH,
        )

    def order_copy():
        return pltpu.make_async_remote_copy(
            order_own, order_next, order_sem.at[0], order_sem.at[1],
            device_id=(me, section - 1), device_id_type=MESH,
        )

    loads = [
        pltpu.make_async_copy(source, target, load_sem.at[i])
        for i, (source, target) in enumerate(
            [
                (x_hbm, x_ref),
                (up_hbm, up_ref),
                (w_hbm, w_ref),
                (wo_hbm, wo_ref),
                (gain_hbm, gain_ref),
                (bias_hbm, bias_ref),
                (send_hbm, send_ref),
                (recv_hbm, recv_ref),
                (len_hbm, len_ref),
            ]
        )
    ]
    barrier = pltpu.get_barrier_semaphore()

    @pl.when(section > 0)
    def _():
        for i in (6, 0, 3, 1, 7, 8, 4, 5, 2):
            loads[i].start()

        def greet(step):
            pl.semaphore_signal(
                barrier, inc=1, device_id=(lax.rem(me + step, n), section), device_id_type=MESH
            )

        each(1, n, greet)

    @pl.when(section < sections - 1)
    def _():
        def greet(step):
            pl.semaphore_signal(
                barrier, inc=1, device_id=(lax.rem(me + step, n), section + 1), device_id_type=MESH
            )

        each(0, n, greet)

    @pl.when(section > 0)
    def _():
        loads[6].wait()
        order_own[...] = jnp.broadcast_to(send_ref[0], order_own.shape)
        row_of = send_ref[0].astype(jnp.float32)
        eye = iota((rows, rows), 0) == iota((rows, rows), 1)
        column = jnp.sum(jnp.where(eye, row_of, 0.0), axis=1, keepdims=True).astype(jnp.int32)
        pick = jnp.where(column == iota((rows, rows), 1), 1.0, 0.0).astype(jnp.bfloat16)
        loads[0].wait()
        send_x[...] = spread(dot(pick, x_ref[0]).astype(jnp.bfloat16))
        pl.semaphore_wait(barrier, 2 * n - 1)
        each(1, n, lambda step: x_copy(lax.rem(me + step, n), me, lax.rem(me + step, n)).start())
        loads[1].wait()
        loads[3].wait()
        out_common = dot_nt(up_ref[0], wo_ref[0]).astype(jnp.bfloat16)
        send_o[...] = spread(dot(pick, out_common).astype(jnp.bfloat16))
        each(1, n, lambda step: o_copy(lax.rem(me + step, n), me, lax.rem(me + step, n)).start())
        up_copy().start()
        order_copy().start()
        recv_x[me] = send_x[me]
        recv_o[me] = send_o[me]

        loads[7].wait()
        loads[8].wait()
        place = iota((1, rows), 1)
        end = jnp.zeros((1, 1), jnp.int32)
        segment = jnp.zeros((1, rows), jnp.float32)
        for patch in range(len_ref.shape[2]):
            end = end + len_ref[0, :, patch : patch + 1]
            segment = segment + jnp.where(place >= end, 1.0, 0.0)
        at = recv_ref[0] == iota((rows, rows), 0)
        patch_of = jnp.sum(jnp.where(at, segment, 0.0), axis=1, keepdims=True).astype(jnp.int32)
        lanes = iota((rows, half), 1)
        feat_k[...] = jnp.where(patch_of == lanes, 1.0, 0.0).astype(jnp.bfloat16)
        feat_q[...] = jnp.where(patch_of == lanes, 0.0, -1e30).astype(jnp.bfloat16)

        for i in (4, 5, 2):
            loads[i].wait()

        def x_wait(step):
            peer = lax.rem(me + step, n)
            x_copy(peer, peer, peer).wait_recv()

        each(1, n, x_wait)
        values = gather(recv_x[...]).astype(jnp.float32)
        centered = values - jnp.mean(values, axis=-1, keepdims=True)
        inverse = lax.rsqrt(jnp.mean(centered * centered, axis=-1, keepdims=True) + 1e-05)
        xhat = centered * inverse
        xhat_ref[...] = xhat
        inverse_ref[...] = jnp.broadcast_to(inverse, inverse_ref.shape)
        normed = (xhat * gain_ref[...] + bias_ref[...]).astype(jnp.bfloat16)
        q_ref[...] = dot(normed, w_ref[0, :, :width]).astype(jnp.bfloat16)
        key = dot(normed, w_ref[0, :, width : 2 * width]).astype(jnp.bfloat16)
        k_ref[...] = key
        kt_ref[...] = key.astype(jnp.float32).T.astype(jnp.bfloat16)
        v_ref[...] = dot(normed, w_ref[0, :, 2 * width :]).astype(jnp.bfloat16)

        rate = float(HEAD) ** (-0.5) * math.log2(math.e)
        lane_head = iota((rows, half), 1) // HEAD
        zero = jnp.zeros((rows, half), jnp.bfloat16)
        groups = half // HEAD // GROUP

        def softmax_heads(part, group):
            columns = slice(part * half, (part + 1) * half)
            query_right = jnp.concatenate([q_ref[:, columns], feat_q[...]], axis=1)
            mine = [lane_head == group * GROUP + i for i in range(GROUP)]
            key, feature = k_ref[:, columns], feat_k[...]
            keys = jnp.concatenate(
                [jnp.concatenate([jnp.where(m, key, zero), feature], axis=1) for m in mine], axis=0
            )
            scores = dot_nt(keys, query_right)
            for i in range(GROUP):
                score = scores[i * rows : (i + 1) * rows]
                expo = jnp.exp2((score - jnp.max(score, axis=0, keepdims=True)) * rate)
                start = pl.multiple_of(((part * groups + group) * GROUP + i) * rows, rows)
                probs_ref[pl.ds(start, rows), :] = expo * (1.0 / jnp.sum(expo, axis=0, keepdims=True))

        def gradient_heads(part, group):
            columns = slice(part * half, (part + 1) * half)
            query, value, dout = q_ref[:, columns], v_ref[:, columns], do_ref[:, columns]
            mine = [lane_head == group * GROUP + i for i in range(GROUP)]
            values = jnp.concatenate([jnp.where(m, value, zero) for m in mine], axis=0)
            dprobs = dot_nt(values, dout)
            weights, dscores = [], []
            for i in range(GROUP):
                start = pl.multiple_of(((part * groups + group) * GROUP + i) * rows, rows)
                probs = probs_ref[pl.ds(start, rows), :]
                dprob = dprobs[i * rows : (i + 1) * rows]
                inner = jnp.sum(dprob * probs, axis=0, keepdims=True)
                weights.append(probs.astype(jnp.bfloat16))
                dscores.append((probs * (dprob - inner)).astype(jnp.bfloat16))
            dkeys = dot(jnp.concatenate(dscores, axis=0), query)
            dvalues = dot(jnp.concatenate(weights, axis=0), dout)
            dkey, dvalue = dk_ref[:, columns], dv_ref[:, columns]
            for i in range(GROUP):
                dkey = jnp.where(mine[i], dkeys[i * rows : (i + 1) * rows], dkey)
                dvalue = jnp.where(mine[i], dvalues[i * rows : (i + 1) * rows], dvalue)
                start = pl.multiple_of(part * half + (group * GROUP + i) * HEAD, HEAD)
                dqt_ref[pl.ds(start, HEAD), :] = dot(kt_ref[pl.ds(start, HEAD), :], dscores[i])
            dk_ref[:, columns] = dkey
            dv_ref[:, columns] = dvalue

        def all_heads(some_heads):
            for part in range(width // half):
                lax.fori_loop(0, groups, lambda group, carry: (some_heads(part, group), carry)[1], 0)

        all_heads(softmax_heads)

        def o_wait(step):
            peer = lax.rem(me + step, n)
            o_copy(peer, peer, peer).wait_recv()

        each(1, n, o_wait)
        do_ref[...] = gather(recv_o[...])
        all_heads(gradient_heads)

        scale = float(HEAD) ** (-0.5)
        dqkv_ref[:, :width] = (dqt_ref[...].T * scale).astype(jnp.bfloat16)
        dqkv_ref[:, width : 2 * width] = (dk_ref[...] * scale).astype(jnp.bfloat16)
        dqkv_ref[:, 2 * width :] = dv_ref[...].astype(jnp.bfloat16)
        pieces = 2 if slot == block and n % 2 == 0 else 1
        peers, few = n // pieces, rows // pieces
        for piece in range(pieces):
            which = lax.rem(me // peers + 1 + piece, pieces)
            some = pl.ds(pl.multiple_of(which * few, few), few)
            grad = dot_nt(dqkv_ref[some, :], w_ref[0]) * gain_ref[...]
            xhat = xhat_ref[some, :]
            mean = jnp.mean(grad, axis=-1, keepdims=True)
            cross = jnp.mean(grad * xhat, axis=-1, keepdims=True)
            branch = (inverse_ref[some, :1] * (grad - mean - xhat * cross)).astype(jnp.bfloat16)
            if pieces == 1:
                send_b[...] = spread(branch)
            else:
                send_b[pl.ds(which * peers, peers)] = branch.reshape(peers, slot, wide)

            def send_back(step, which=which):
                peer = which * peers + lax.rem(me + step, peers)
                b_copy(peer, me, peer).start()

            each(0, peers, send_back)

    @pl.when(section < sections - 1)
    def _():
        order_copy().wait_recv()
        up_copy().wait_recv()
        pick = jnp.where(order_next[0:1, :] == iota((rows, rows), 0), 1.0, 0.0).astype(jnp.bfloat16)

        def b_wait(step):
            peer = lax.rem(me + step, n)
            b_copy(peer, peer, peer).wait_recv()

        each(0, n, b_wait)
        branch = dot(pick, gather(recv_b[...]))
        out_ref[0] = (up_next[...].astype(jnp.float32) + branch).astype(jnp.bfloat16)

    @pl.when(section == sections - 1)
    def _():
        out_ref[...] = jnp.zeros_like(out_ref)

    @pl.when(section > 0)
    def _():
        def sent(step):
            peer = lax.rem(me + step, n)
            x_copy(peer, me, peer).wait_send()
            o_copy(peer, me, peer).wait_send()

        each(1, n, sent)

        def sent_back(step):
            peer = lax.rem(me + step, n)
            b_copy(peer, me, peer).wait_send()

        each(0, n, sent_back)
        up_copy().wait_send()
        order_copy().wait_send()


def per_device(x, up, w_qkv, w_out, gain, bias, send_order, recv_order, lengths):
    n, sections = lax.axis_size("seq"), lax.axis_size("section")
    rows, wide = x.shape[1], x.shape[2]
    width = w_out.shape[1]
    slot = max(rows // n, 16)
    vmem = pl.BlockSpec(memory_space=pltpu.VMEM)
    bf16, f32 = jnp.bfloat16, jnp.float32
    dma = pltpu.SemaphoreType.DMA
    operands = (x, up, w_qkv, w_out, gain, bias, send_order, recv_order, lengths)
    return pl.pallas_call(
        functools.partial(kernel, n, sections),
        out_shape=jax.ShapeDtypeStruct(x.shape, bf16),
        in_specs=[pl.BlockSpec(memory_space=pltpu.HBM)] * 9,
        out_specs=vmem,
        scratch_shapes=[
            *[pltpu.VMEM(a.shape, a.dtype) for a in operands],
            dma((len(operands),)),
            pltpu.VMEM((n, slot, wide), bf16),
            pltpu.VMEM((n, slot, wide), bf16),
            pltpu.VMEM((n, slot, width), bf16),
            pltpu.VMEM((n, slot, width), bf16),
            pltpu.VMEM((n, slot, wide), bf16),
            pltpu.VMEM((n, slot, wide), bf16),
            pltpu.VMEM((rows, wide), bf16),
            pltpu.VMEM((8, rows), jnp.int32),
            pltpu.VMEM((8, rows), jnp.int32),
            pltpu.VMEM((rows, wide), f32),
            pltpu.VMEM((rows, width), bf16),
            pltpu.VMEM((rows, width), bf16),
            pltpu.VMEM((rows, width), bf16),
            pltpu.VMEM((width, rows), bf16),
            pltpu.VMEM((rows, width), bf16),
            pltpu.VMEM((rows, 128), bf16),
            pltpu.VMEM((rows, 128), bf16),
            pltpu.VMEM((width, rows), f32),
            pltpu.VMEM((width // HEAD * rows, rows), f32),
            pltpu.VMEM((rows, 3 * width), bf16),
            pltpu.VMEM((rows, 128), f32),
            pltpu.VMEM((rows, width), f32),
            pltpu.VMEM((rows, width), f32),
            dma((n,)),
            dma((n,)),
            dma((n,)),
            dma((n,)),
            dma((n,)),
            dma((n,)),
            dma((2,)),
            dma((2,)),
        ],
        compiler_params=pltpu.CompilerParams(
            collective_id=0, has_side_effects=True, vmem_limit_bytes=62 * 1024 * 1024
        ),
        name="patch_attention_grad",
    )(*operands)


def solution(mesh):
    return jax.shard_map(
        per_device,
        mesh=mesh,
        in_specs=(
            P("section", "seq", None),
            P("section", "seq", None),
            P("section", None, None),
            P("section", None, None),
            P("section", None),
            P("section", None),
            P("section", "seq", None),
            P("section", "seq", None),
            P("section", "seq", None),
        ),
        out_specs=P("section", "seq", None),
        check_vma=False,
    )
```

```python
import functools
import math

import jax
import jax.numpy as jnp
from jax import lax
from jax.experimental import pallas as pl
from jax.experimental.pallas import tpu as pltpu
from jax.sharding import PartitionSpec as P

HEAD = 16
MESH = pl.DeviceIdType.MESH
LAST = (((1,), (1,)), ((), ()))
GROUP = 4


def dot(a, b):
    return jnp.dot(a, b, preferred_element_type=jnp.float32)


def dot_nt(a, b):
    return lax.dot_general(a, b, LAST, preferred_element_type=jnp.float32)


def each(first, count, body):
    if count - first <= 8:
        for step in by_distance(first, count):
            body(step)
    else:
        lax.fori_loop(first, count, lambda step, carry: (body(step), carry)[1], 0)


def by_distance(first, count):
    return sorted(range(first, count), key=lambda step: (abs(step - count // 2), step))


def iota(shape, axis):
    return lax.broadcasted_iota(jnp.int32, shape, axis)


def kernel(
    n,
    sections,
    x_hbm,
    up_hbm,
    w_hbm,
    wo_hbm,
    gain_hbm,
    bias_hbm,
    send_hbm,
    recv_hbm,
    len_hbm,
    out_ref,
    x_ref,
    up_ref,
    w_ref,
    wo_ref,
    gain_ref,
    bias_ref,
    send_ref,
    recv_ref,
    len_ref,
    load_sem,
    send_x,
    recv_x,
    send_o,
    recv_o,
    send_b,
    recv_b,
    up_next,
    order_own,
    order_next,
    xhat_ref,
    q_ref,
    k_ref,
    v_ref,
    kt_ref,
    do_ref,
    feat_q,
    feat_k,
    dqt_ref,
    probs_ref,
    dqkv_ref,
    inverse_ref,
    dk_ref,
    dv_ref,
    sx_sem,
    rx_sem,
    so_sem,
    ro_sem,
    sb_sem,
    rb_sem,
    up_sem,
    order_sem,
):
    me = lax.axis_index("seq")
    section = lax.axis_index("section")
    rows, wide = x_ref.shape[1], x_ref.shape[2]
    width = wo_ref.shape[1]
    slot = send_x.shape[1]
    block = rows // n
    half = 128

    def spread(values):
        if slot == block:
            return values.reshape(n, slot, values.shape[1])
        place = iota((n * slot, rows), 0)
        source = jnp.where(place % slot < block, place // slot * block + place % slot, -1)
        pick = (source == iota((n * slot, rows), 1)).astype(jnp.bfloat16)
        return dot(pick, values).astype(jnp.bfloat16).reshape(n, slot, values.shape[1])

    def gather(values):
        values = values.reshape(n * slot, values.shape[2])
        if slot == block:
            return values
        place = iota((rows, n * slot), 0)
        pick = (place // block * slot + place % block == iota((rows, n * slot), 1)).astype(jnp.bfloat16)
        return dot(pick, values).astype(jnp.bfloat16)

    def x_copy(local, there, peer):
        return pltpu.make_async_remote_copy(
            send_x.at[local], recv_x.at[there], sx_sem.at[local], rx_sem.at[there],
            device_id=(peer, section), device_id_type=MESH,
        )

    def o_copy(local, there, peer):
        return pltpu.make_async_remote_copy(
            send_o.at[local], recv_o.at[there], so_sem.at[local], ro_sem.at[there],
            device_id=(peer, section), device_id_type=MESH,
        )

    def b_copy(local, there, peer):
        return pltpu.make_async_remote_copy(
            send_b.at[local], recv_b.at[there], sb_sem.at[local], rb_sem.at[there],
            device_id=(peer, section - 1), device_id_type=MESH,
        )

    def up_copy():
        return pltpu.make_async_remote_copy(
            up_ref.at[0], up_next, up_sem.at[0], up_sem.at[1],
            device_id=(me, section - 1), device_id_type=MESH,
        )

    def order_copy():
        return pltpu.make_async_remote_copy(
            order_own, order_next, order_sem.at[0], order_sem.at[1],
            device_id=(me, section - 1), device_id_type=MESH,
        )

    loads = [
        pltpu.make_async_copy(source, target, load_sem.at[i])
        for i, (source, target) in enumerate(
            [
                (x_hbm, x_ref),
                (up_hbm, up_ref),
                (w_hbm, w_ref),
                (wo_hbm, wo_ref),
                (gain_hbm, gain_ref),
                (bias_hbm, bias_ref),
                (send_hbm, send_ref),
                (recv_hbm, recv_ref),
                (len_hbm, len_ref),
            ]
        )
    ]
    barrier = pltpu.get_barrier_semaphore()

    @pl.when(section > 0)
    def _():
        for i in (6, 0, 3, 1, 7, 8, 4, 5, 2):
            loads[i].start()

        def greet(step):
            pl.semaphore_signal(
                barrier, inc=1, device_id=(lax.rem(me + step, n), section), device_id_type=MESH
            )

        each(1, n, greet)

    @pl.when(section < sections - 1)
    def _():
        def greet(step):
            pl.semaphore_signal(
                barrier, inc=1, device_id=(lax.rem(me + step, n), section + 1), device_id_type=MESH
            )

        each(0, n, greet)

    @pl.when(section > 0)
    def _():
        loads[6].wait()
        order_own[...] = jnp.broadcast_to(send_ref[0], order_own.shape)
        row_of = send_ref[0].astype(jnp.float32)
        eye = iota((rows, rows), 0) == iota((rows, rows), 1)
        column = jnp.sum(jnp.where(eye, row_of, 0.0), axis=1, keepdims=True).astype(jnp.int32)
        pick = jnp.where(column == iota((rows, rows), 1), 1.0, 0.0).astype(jnp.bfloat16)
        loads[0].wait()
        send_x[...] = spread(dot(pick, x_ref[0]).astype(jnp.bfloat16))
        pl.semaphore_wait(barrier, 2 * n - 1)
        each(1, n, lambda step: x_copy(lax.rem(me + step, n), me, lax.rem(me + step, n)).start())
        loads[1].wait()
        loads[3].wait()
        out_common = dot_nt(up_ref[0], wo_ref[0]).astype(jnp.bfloat16)
        send_o[...] = spread(dot(pick, out_common).astype(jnp.bfloat16))
        each(1, n, lambda step: o_copy(lax.rem(me + step, n), me, lax.rem(me + step, n)).start())
        up_copy().start()
        order_copy().start()
        recv_x[me] = send_x[me]
        recv_o[me] = send_o[me]

        loads[7].wait()
        loads[8].wait()
        place = iota((1, rows), 1)
        end = jnp.zeros((1, 1), jnp.int32)
        segment = jnp.zeros((1, rows), jnp.float32)
        for patch in range(len_ref.shape[2]):
            end = end + len_ref[0, :, patch : patch + 1]
            segment = segment + jnp.where(place >= end, 1.0, 0.0)
        at = recv_ref[0] == iota((rows, rows), 0)
        patch_of = jnp.sum(jnp.where(at, segment, 0.0), axis=1, keepdims=True).astype(jnp.int32)
        lanes = iota((rows, half), 1)
        feat_k[...] = jnp.where(patch_of == lanes, 1.0, 0.0).astype(jnp.bfloat16)
        feat_q[...] = jnp.where(patch_of == lanes, 0.0, -1e30).astype(jnp.bfloat16)

        for i in (4, 5, 2):
            loads[i].wait()

        def x_wait(step):
            peer = lax.rem(me + step, n)
            x_copy(peer, peer, peer).wait_recv()

        each(1, n, x_wait)
        values = gather(recv_x[...]).astype(jnp.float32)
        centered = values - jnp.mean(values, axis=-1, keepdims=True)
        inverse = lax.rsqrt(jnp.mean(centered * centered, axis=-1, keepdims=True) + 1e-05)
        xhat = centered * inverse
        xhat_ref[...] = xhat
        inverse_ref[...] = jnp.broadcast_to(inverse, inverse_ref.shape)
        normed = (xhat * gain_ref[...] + bias_ref[...]).astype(jnp.bfloat16)
        q_ref[...] = dot(normed, w_ref[0, :, :width]).astype(jnp.bfloat16)
        key = dot(normed, w_ref[0, :, width : 2 * width]).astype(jnp.bfloat16)
        k_ref[...] = key
        kt_ref[...] = key.astype(jnp.float32).T.astype(jnp.bfloat16)
        v_ref[...] = dot(normed, w_ref[0, :, 2 * width :]).astype(jnp.bfloat16)

        rate = float(HEAD) ** (-0.5) * math.log2(math.e)
        lane_head = iota((rows, half), 1) // HEAD
        zero = jnp.zeros((rows, half), jnp.bfloat16)
        groups = half // HEAD // GROUP

        def softmax_heads(part, group):
            columns = slice(part * half, (part + 1) * half)
            query_right = jnp.concatenate([q_ref[:, columns], feat_q[...]], axis=1)
            mine = [lane_head == group * GROUP + i for i in range(GROUP)]
            key, feature = k_ref[:, columns], feat_k[...]
            keys = jnp.concatenate(
                [jnp.concatenate([jnp.where(m, key, zero), feature], axis=1) for m in mine], axis=0
            )
            scores = dot_nt(keys, query_right)
            for i in range(GROUP):
                score = scores[i * rows : (i + 1) * rows]
                expo = jnp.exp2((score - jnp.max(score, axis=0, keepdims=True)) * rate)
                start = pl.multiple_of(((part * groups + group) * GROUP + i) * rows, rows)
                probs_ref[pl.ds(start, rows), :] = expo * (1.0 / jnp.sum(expo, axis=0, keepdims=True))

        def gradient_heads(part, group):
            columns = slice(part * half, (part + 1) * half)
            query, value, dout = q_ref[:, columns], v_ref[:, columns], do_ref[:, columns]
            mine = [lane_head == group * GROUP + i for i in range(GROUP)]
            values = jnp.concatenate([jnp.where(m, value, zero) for m in mine], axis=0)
            dprobs = dot_nt(values, dout)
            weights, dscores = [], []
            for i in range(GROUP):
                start = pl.multiple_of(((part * groups + group) * GROUP + i) * rows, rows)
                probs = probs_ref[pl.ds(start, rows), :]
                dprob = dprobs[i * rows : (i + 1) * rows]
                inner = jnp.sum(dprob * probs, axis=0, keepdims=True)
                weights.append(probs.astype(jnp.bfloat16))
                dscores.append((probs * (dprob - inner)).astype(jnp.bfloat16))
            dkeys = dot(jnp.concatenate(dscores, axis=0), query)
            dvalues = dot(jnp.concatenate(weights, axis=0), dout)
            dkey, dvalue = dk_ref[:, columns], dv_ref[:, columns]
            for i in range(GROUP):
                dkey = jnp.where(mine[i], dkeys[i * rows : (i + 1) * rows], dkey)
                dvalue = jnp.where(mine[i], dvalues[i * rows : (i + 1) * rows], dvalue)
                start = pl.multiple_of(part * half + (group * GROUP + i) * HEAD, HEAD)
                dqt_ref[pl.ds(start, HEAD), :] = dot(kt_ref[pl.ds(start, HEAD), :], dscores[i])
            dk_ref[:, columns] = dkey
            dv_ref[:, columns] = dvalue

        def all_heads(some_heads):
            for part in range(width // half):
                lax.fori_loop(0, groups, lambda group, carry: (some_heads(part, group), carry)[1], 0)

        all_heads(softmax_heads)

        def o_wait(step):
            peer = lax.rem(me + step, n)
            o_copy(peer, peer, peer).wait_recv()

        each(1, n, o_wait)
        do_ref[...] = gather(recv_o[...])
        all_heads(gradient_heads)

        scale = float(HEAD) ** (-0.5)
        dqkv_ref[:, :width] = (dqt_ref[...].T * scale).astype(jnp.bfloat16)
        dqkv_ref[:, width : 2 * width] = (dk_ref[...] * scale).astype(jnp.bfloat16)
        dqkv_ref[:, 2 * width :] = dv_ref[...].astype(jnp.bfloat16)
        pieces = 2 if slot == block and n % 2 == 0 else 1
        peers, few = n // pieces, rows // pieces
        for piece in range(pieces):
            which = lax.rem(me // peers + 1 + piece, pieces)
            some = pl.ds(pl.multiple_of(which * few, few), few)
            grad = dot_nt(dqkv_ref[some, :], w_ref[0]) * gain_ref[...]
            xhat = xhat_ref[some, :]
            mean = jnp.mean(grad, axis=-1, keepdims=True)
            cross = jnp.mean(grad * xhat, axis=-1, keepdims=True)
            branch = (inverse_ref[some, :1] * (grad - mean - xhat * cross)).astype(jnp.bfloat16)
            if pieces == 1:
                send_b[...] = spread(branch)
            else:
                send_b[pl.ds(which * peers, peers)] = branch.reshape(peers, slot, wide)

            def send_back(step, which=which):
                peer = which * peers + lax.rem(me + step, peers)
                b_copy(peer, me, peer).start()

            each(0, peers, send_back)

    @pl.when(section < sections - 1)
    def _():
        order_copy().wait_recv()
        up_copy().wait_recv()
        pick = jnp.where(order_next[0:1, :] == iota((rows, rows), 0), 1.0, 0.0).astype(jnp.bfloat16)

        def b_wait(step):
            peer = lax.rem(me + step, n)
            b_copy(peer, peer, peer).wait_recv()

        each(0, n, b_wait)
        branch = dot(pick, gather(recv_b[...]))
        out_ref[0] = (up_next[...].astype(jnp.float32) + branch).astype(jnp.bfloat16)

    @pl.when(section == sections - 1)
    def _():
        out_ref[...] = jnp.zeros_like(out_ref)

    @pl.when(section > 0)
    def _():
        def sent(step):
            peer = lax.rem(me + step, n)
            x_copy(peer, me, peer).wait_send()
            o_copy(peer, me, peer).wait_send()

        each(1, n, sent)

        def sent_back(step):
            peer = lax.rem(me + step, n)
            b_copy(peer, me, peer).wait_send()

        each(0, n, sent_back)
        up_copy().wait_send()
        order_copy().wait_send()


def per_device(x, up, w_qkv, w_out, gain, bias, send_order, recv_order, lengths):
    n, sections = lax.axis_size("seq"), lax.axis_size("section")
    rows, wide = x.shape[1], x.shape[2]
    width = w_out.shape[1]
    slot = max(rows // n, 16)
    vmem = pl.BlockSpec(memory_space=pltpu.VMEM)
    bf16, f32 = jnp.bfloat16, jnp.float32
    dma = pltpu.SemaphoreType.DMA
    operands = (x, up, w_qkv, w_out, gain, bias, send_order, recv_order, lengths)
    operands = [pltpu.with_memory_space_constraint(a, pltpu.HBM) for a in operands]
    return pl.pallas_call(
        functools.partial(kernel, n, sections),
        out_shape=jax.ShapeDtypeStruct(x.shape, bf16),
        in_specs=[pl.BlockSpec(memory_space=pltpu.HBM)] * 9,
        out_specs=vmem,
        scratch_shapes=[
            *[pltpu.VMEM(a.shape, a.dtype) for a in operands],
            dma((len(operands),)),
            pltpu.VMEM((n, slot, wide), bf16),
            pltpu.VMEM((n, slot, wide), bf16),
            pltpu.VMEM((n, slot, width), bf16),
            pltpu.VMEM((n, slot, width), bf16),
            pltpu.VMEM((n, slot, wide), bf16),
            pltpu.VMEM((n, slot, wide), bf16),
            pltpu.VMEM((rows, wide), bf16),
            pltpu.VMEM((8, rows), jnp.int32),
            pltpu.VMEM((8, rows), jnp.int32),
            pltpu.VMEM((rows, wide), f32),
            pltpu.VMEM((rows, width), bf16),
            pltpu.VMEM((rows, width), bf16),
            pltpu.VMEM((rows, width), bf16),
            pltpu.VMEM((width, rows), bf16),
            pltpu.VMEM((rows, width), bf16),
            pltpu.VMEM((rows, 128), bf16),
            pltpu.VMEM((rows, 128), bf16),
            pltpu.VMEM((width, rows), f32),
            pltpu.VMEM((width // HEAD * rows, rows), f32),
            pltpu.VMEM((rows, 3 * width), bf16),
            pltpu.VMEM((rows, 128), f32),
            pltpu.VMEM((rows, width), f32),
            pltpu.VMEM((rows, width), f32),
            dma((n,)),
            dma((n,)),
            dma((n,)),
            dma((n,)),
            dma((n,)),
            dma((n,)),
            dma((2,)),
            dma((2,)),
        ],
        compiler_params=pltpu.CompilerParams(
            collective_id=0, has_side_effects=True, vmem_limit_bytes=40 * 1024 * 1024
        ),
        name="patch_attention_grad",
    )(*operands)


def solution(mesh):
    return jax.shard_map(
        per_device,
        mesh=mesh,
        in_specs=(
            P("section", "seq", None),
            P("section", "seq", None),
            P("section", None, None),
            P("section", None, None),
            P("section", None),
            P("section", None),
            P("section", "seq", None),
            P("section", "seq", None),
            P("section", "seq", None),
        ),
        out_specs=P("section", "seq", None),
        check_vma=False,
    )
```

```python
import functools
import math

import jax
import jax.numpy as jnp
from jax import lax
from jax.experimental import pallas as pl
from jax.experimental.pallas import tpu as pltpu
from jax.sharding import PartitionSpec as P

HEAD = 16
MESH = pl.DeviceIdType.MESH
LAST = (((1,), (1,)), ((), ()))
GROUP = 4


def dot(a, b):
    return jnp.dot(a, b, preferred_element_type=jnp.float32)


def dot_nt(a, b):
    return lax.dot_general(a, b, LAST, preferred_element_type=jnp.float32)


def each(first, count, body):
    if count - first <= 8:
        for step in by_distance(first, count):
            body(step)
    else:
        lax.fori_loop(first, count, lambda step, carry: (body(step), carry)[1], 0)


def by_distance(first, count):
    return sorted(range(first, count), key=lambda step: (abs(step - count // 2), step))


def iota(shape, axis):
    return lax.broadcasted_iota(jnp.int32, shape, axis)


def kernel(
    n,
    sections,
    paired,
    x_hbm,
    up_hbm,
    w_hbm,
    wo_hbm,
    gain_hbm,
    bias_hbm,
    send_hbm,
    recv_hbm,
    len_hbm,
    out_ref,
    x_ref,
    up_ref,
    w_ref,
    wo_ref,
    gain_ref,
    bias_ref,
    send_ref,
    recv_ref,
    len_ref,
    load_sem,
    send_x,
    recv_x,
    send_o,
    recv_o,
    send_b,
    recv_b,
    up_next,
    order_own,
    order_next,
    xhat_ref,
    q_ref,
    k_ref,
    v_ref,
    kt_ref,
    do_ref,
    feat_q,
    feat_k,
    dqt_ref,
    probs_ref,
    dqkv_ref,
    inverse_ref,
    dk_ref,
    dv_ref,
    sx_sem,
    rx_sem,
    so_sem,
    ro_sem,
    sb_sem,
    rb_sem,
    up_sem,
    order_sem,
    turn_sem,
):
    me = lax.axis_index("seq")
    section = lax.axis_index("section")
    rows, wide = x_ref.shape[1], x_ref.shape[2]
    width = wo_ref.shape[1]
    slot = send_x.shape[1]
    block = rows // n
    half = 128

    def spread(values):
        if slot == block:
            return values.reshape(n, slot, values.shape[1])
        place = iota((n * slot, rows), 0)
        source = jnp.where(place % slot < block, place // slot * block + place % slot, -1)
        pick = (source == iota((n * slot, rows), 1)).astype(jnp.bfloat16)
        return dot(pick, values).astype(jnp.bfloat16).reshape(n, slot, values.shape[1])

    def gather(values):
        values = values.reshape(n * slot, values.shape[2])
        if slot == block:
            return values
        place = iota((rows, n * slot), 0)
        pick = (place // block * slot + place % block == iota((rows, n * slot), 1)).astype(jnp.bfloat16)
        return dot(pick, values).astype(jnp.bfloat16)

    def x_copy(local, there, peer):
        return pltpu.make_async_remote_copy(
            send_x.at[local], recv_x.at[there], sx_sem.at[local], rx_sem.at[there],
            device_id=(peer, section), device_id_type=MESH,
        )

    def o_copy(local, there, peer):
        return pltpu.make_async_remote_copy(
            send_o.at[local], recv_o.at[there], so_sem.at[local], ro_sem.at[there],
            device_id=(peer, section), device_id_type=MESH,
        )

    def b_copy(local, there, peer):
        return pltpu.make_async_remote_copy(
            send_b.at[local], recv_b.at[there], sb_sem.at[local], rb_sem.at[there],
            device_id=(peer, section - 1), device_id_type=MESH,
        )

    def up_copy():
        return pltpu.make_async_remote_copy(
            up_ref.at[0], up_next, up_sem.at[0], up_sem.at[1],
            device_id=(me, section - 1), device_id_type=MESH,
        )

    def order_copy():
        return pltpu.make_async_remote_copy(
            order_own, order_next, order_sem.at[0], order_sem.at[1],
            device_id=(me, section - 1), device_id_type=MESH,
        )

    loads = [
        pltpu.make_async_copy(source, target, load_sem.at[i])
        for i, (source, target) in enumerate(
            [
                (x_hbm, x_ref),
                (up_hbm, up_ref),
                (w_hbm, w_ref),
                (wo_hbm, wo_ref),
                (gain_hbm, gain_ref),
                (bias_hbm, bias_ref),
                (send_hbm, send_ref),
                (recv_hbm, recv_ref),
                (len_hbm, len_ref),
            ]
        )
    ]
    barrier = pltpu.get_barrier_semaphore()

    @pl.when(section > 0)
    def _():
        for i in (6, 0, 3, 1, 7, 8, 4, 5, 2):
            loads[i].start()

        def greet(step):
            pl.semaphore_signal(
                barrier, inc=1, device_id=(lax.rem(me + step, n), section), device_id_type=MESH
            )

        each(1, n, greet)

    @pl.when(section < sections - 1)
    def _():
        def greet(step):
            pl.semaphore_signal(
                barrier, inc=1, device_id=(lax.rem(me + step, n), section + 1), device_id_type=MESH
            )

        each(0, n, greet)

    first_of_pair = (section % 2 == 0) & (section > 0)
    second_of_pair = (section % 2 == 1) & (section > 1)
    if paired:

        @pl.when(second_of_pair)
        def _():
            pl.semaphore_signal(barrier, inc=1, device_id=(me, section - 1), device_id_type=MESH)

    @pl.when(section > 0)
    def _():
        loads[6].wait()
        order_own[...] = jnp.broadcast_to(send_ref[0], order_own.shape)
        row_of = send_ref[0].astype(jnp.float32)
        eye = iota((rows, rows), 0) == iota((rows, rows), 1)
        column = jnp.sum(jnp.where(eye, row_of, 0.0), axis=1, keepdims=True).astype(jnp.int32)
        pick = jnp.where(column == iota((rows, rows), 1), 1.0, 0.0).astype(jnp.bfloat16)
        loads[0].wait()
        send_x[...] = spread(dot(pick, x_ref[0]).astype(jnp.bfloat16))
        greetings = 2 * n - 1
        if paired:
            greetings = greetings + first_of_pair.astype(jnp.int32)
        pl.semaphore_wait(barrier, greetings)
        if paired:

            @pl.when(second_of_pair)
            def _():
                pl.semaphore_wait(turn_sem, 1)

        each(1, n, lambda step: x_copy(lax.rem(me + step, n), me, lax.rem(me + step, n)).start())
        loads[1].wait()
        loads[3].wait()
        out_common = dot_nt(up_ref[0], wo_ref[0]).astype(jnp.bfloat16)
        send_o[...] = spread(dot(pick, out_common).astype(jnp.bfloat16))
        recv_x[me] = send_x[me]
        recv_o[me] = send_o[me]

        loads[7].wait()
        loads[8].wait()
        place = iota((1, rows), 1)
        end = jnp.zeros((1, 1), jnp.int32)
        segment = jnp.zeros((1, rows), jnp.float32)
        for patch in range(len_ref.shape[2]):
            end = end + len_ref[0, :, patch : patch + 1]
            segment = segment + jnp.where(place >= end, 1.0, 0.0)
        at = recv_ref[0] == iota((rows, rows), 0)
        patch_of = jnp.sum(jnp.where(at, segment, 0.0), axis=1, keepdims=True).astype(jnp.int32)
        lanes = iota((rows, half), 1)
        feat_k[...] = jnp.where(patch_of == lanes, 1.0, 0.0).astype(jnp.bfloat16)
        feat_q[...] = jnp.where(patch_of == lanes, 0.0, -1e30).astype(jnp.bfloat16)

        for i in (4, 5, 2):
            loads[i].wait()

        def x_sent(step):
            peer = lax.rem(me + step, n)
            x_copy(peer, me, peer).wait_send()

        each(1, n, x_sent)
        if paired:

            @pl.when(first_of_pair)
            def _():
                pl.semaphore_signal(turn_sem, inc=1, device_id=(me, section + 1), device_id_type=MESH)

        def x_wait(step):
            peer = lax.rem(me + step, n)
            x_copy(peer, peer, peer).wait_recv()

        each(1, n, x_wait)
        values = gather(recv_x[...]).astype(jnp.float32)
        centered = values - jnp.mean(values, axis=-1, keepdims=True)
        inverse = lax.rsqrt(jnp.mean(centered * centered, axis=-1, keepdims=True) + 1e-05)
        xhat = centered * inverse
        xhat_ref[...] = xhat
        inverse_ref[...] = jnp.broadcast_to(inverse, inverse_ref.shape)
        normed = (xhat * gain_ref[...] + bias_ref[...]).astype(jnp.bfloat16)
        q_ref[...] = dot(normed, w_ref[0, :, :width]).astype(jnp.bfloat16)
        key = dot(normed, w_ref[0, :, width : 2 * width]).astype(jnp.bfloat16)
        k_ref[...] = key
        kt_ref[...] = key.astype(jnp.float32).T.astype(jnp.bfloat16)
        v_ref[...] = dot(normed, w_ref[0, :, 2 * width :]).astype(jnp.bfloat16)

        each(1, n, lambda step: o_copy(lax.rem(me + step, n), me, lax.rem(me + step, n)).start())
        up_copy().start()
        order_copy().start()

        rate = float(HEAD) ** (-0.5) * math.log2(math.e)
        lane_head = iota((rows, half), 1) // HEAD
        zero = jnp.zeros((rows, half), jnp.bfloat16)
        groups = half // HEAD // GROUP

        def softmax_heads(part, group):
            columns = slice(part * half, (part + 1) * half)
            query_right = jnp.concatenate([q_ref[:, columns], feat_q[...]], axis=1)
            mine = [lane_head == group * GROUP + i for i in range(GROUP)]
            key, feature = k_ref[:, columns], feat_k[...]
            keys = jnp.concatenate(
                [jnp.concatenate([jnp.where(m, key, zero), feature], axis=1) for m in mine], axis=0
            )
            scores = dot_nt(keys, query_right)
            for i in range(GROUP):
                start = pl.multiple_of(((part * groups + group) * GROUP + i) * rows, rows)
                for first in range(0, rows, half):
                    some = slice(first, first + half)
                    score = scores[i * rows : (i + 1) * rows, some]
                    expo = jnp.exp2((score - jnp.max(score, axis=0, keepdims=True)) * rate)
                    probs_ref[pl.ds(start, rows), some] = expo * (1.0 / jnp.sum(expo, axis=0, keepdims=True))

        def gradient_heads(part, group):
            columns = slice(part * half, (part + 1) * half)
            query, value, dout = q_ref[:, columns], v_ref[:, columns], do_ref[:, columns]
            mine = [lane_head == group * GROUP + i for i in range(GROUP)]
            values = jnp.concatenate([jnp.where(m, value, zero) for m in mine], axis=0)
            dprobs = dot_nt(values, dout)
            weights, dscores = [], []
            for i in range(GROUP):
                start = pl.multiple_of(((part * groups + group) * GROUP + i) * rows, rows)
                weight, dscore = [], []
                for first in range(0, rows, half):
                    some = slice(first, first + half)
                    probs = probs_ref[pl.ds(start, rows), some]
                    dprob = dprobs[i * rows : (i + 1) * rows, some]
                    inner = jnp.sum(dprob * probs, axis=0, keepdims=True)
                    weight.append(probs.astype(jnp.bfloat16))
                    dscore.append((probs * (dprob - inner)).astype(jnp.bfloat16))
                weights.append(jnp.concatenate(weight, axis=1))
                dscores.append(jnp.concatenate(dscore, axis=1))
            dkeys = dot(jnp.concatenate(dscores, axis=0), query)
            dvalues = dot(jnp.concatenate(weights, axis=0), dout)
            dkey, dvalue = dk_ref[:, columns], dv_ref[:, columns]
            for i in range(GROUP):
                dkey = jnp.where(mine[i], dkeys[i * rows : (i + 1) * rows], dkey)
                dvalue = jnp.where(mine[i], dvalues[i * rows : (i + 1) * rows], dvalue)
                start = pl.multiple_of(part * half + (group * GROUP + i) * HEAD, HEAD)
                dqt_ref[pl.ds(start, HEAD), :] = dot(kt_ref[pl.ds(start, HEAD), :], dscores[i])
            dk_ref[:, columns] = dkey
            dv_ref[:, columns] = dvalue

        def all_heads(some_heads):
            for part in range(width // half):
                lax.fori_loop(0, groups, lambda group, carry: (some_heads(part, group), carry)[1], 0)

        all_heads(softmax_heads)

        def o_wait(step):
            peer = lax.rem(me + step, n)
            o_copy(peer, peer, peer).wait_recv()

        each(1, n, o_wait)
        do_ref[...] = gather(recv_o[...])
        all_heads(gradient_heads)

        scale = float(HEAD) ** (-0.5)
        dqkv_ref[:, :width] = (dqt_ref[...].T * scale).astype(jnp.bfloat16)
        dqkv_ref[:, width : 2 * width] = (dk_ref[...] * scale).astype(jnp.bfloat16)
        dqkv_ref[:, 2 * width :] = dv_ref[...].astype(jnp.bfloat16)
        pieces = 2 if slot == block and n % 2 == 0 else 1
        peers, few = n // pieces, rows // pieces
        for piece in range(pieces):
            which = lax.rem(me // peers + 1 + piece, pieces)
            some = pl.ds(pl.multiple_of(which * few, few), few)
            grad = dot_nt(dqkv_ref[some, :], w_ref[0]) * gain_ref[...]
            xhat = xhat_ref[some, :]
            mean = jnp.mean(grad, axis=-1, keepdims=True)
            cross = jnp.mean(grad * xhat, axis=-1, keepdims=True)
            branch = (inverse_ref[some, :1] * (grad - mean - xhat * cross)).astype(jnp.bfloat16)
            if pieces == 1:
                send_b[...] = spread(branch)
            else:
                send_b[pl.ds(which * peers, peers)] = branch.reshape(peers, slot, wide)

            def send_back(step, which=which):
                peer = which * peers + lax.rem(me + step, peers)
                b_copy(peer, me, peer).start()

            each(0, peers, send_back)

    @pl.when(section < sections - 1)
    def _():
        order_copy().wait_recv()
        up_copy().wait_recv()
        pick = jnp.where(order_next[0:1, :] == iota((rows, rows), 0), 1.0, 0.0).astype(jnp.bfloat16)

        def b_wait(step):
            peer = lax.rem(me + step, n)
            b_copy(peer, peer, peer).wait_recv()

        each(0, n, b_wait)
        branch = dot(pick, gather(recv_b[...]))
        out_ref[0] = (up_next[...].astype(jnp.float32) + branch).astype(jnp.bfloat16)

    @pl.when(section == sections - 1)
    def _():
        out_ref[...] = jnp.zeros_like(out_ref)

    @pl.when(section > 0)
    def _():
        def sent(step):
            peer = lax.rem(me + step, n)
            o_copy(peer, me, peer).wait_send()

        each(1, n, sent)

        def sent_back(step):
            peer = lax.rem(me + step, n)
            b_copy(peer, me, peer).wait_send()

        each(0, n, sent_back)
        up_copy().wait_send()
        order_copy().wait_send()


def per_device(x, up, w_qkv, w_out, gain, bias, send_order, recv_order, lengths):
    n, sections = lax.axis_size("seq"), lax.axis_size("section")
    rows, wide = x.shape[1], x.shape[2]
    width = w_out.shape[1]
    slot = max(rows // n, 16)
    vmem = pl.BlockSpec(memory_space=pltpu.VMEM)
    bf16, f32 = jnp.bfloat16, jnp.float32
    dma = pltpu.SemaphoreType.DMA
    operands = (x, up, w_qkv, w_out, gain, bias, send_order, recv_order, lengths)
    operands = [pltpu.with_memory_space_constraint(a, pltpu.HBM) for a in operands]
    return pl.pallas_call(
        functools.partial(kernel, n, sections, sections % 2 == 0 and n <= 8),
        out_shape=jax.ShapeDtypeStruct(x.shape, bf16),
        in_specs=[pl.BlockSpec(memory_space=pltpu.HBM)] * 9,
        out_specs=vmem,
        scratch_shapes=[
            *[pltpu.VMEM(a.shape, a.dtype) for a in operands],
            dma((len(operands),)),
            pltpu.VMEM((n, slot, wide), bf16),
            pltpu.VMEM((n, slot, wide), bf16),
            pltpu.VMEM((n, slot, width), bf16),
            pltpu.VMEM((n, slot, width), bf16),
            pltpu.VMEM((n, slot, wide), bf16),
            pltpu.VMEM((n, slot, wide), bf16),
            pltpu.VMEM((rows, wide), bf16),
            pltpu.VMEM((8, rows), jnp.int32),
            pltpu.VMEM((8, rows), jnp.int32),
            pltpu.VMEM((rows, wide), f32),
            pltpu.VMEM((rows, width), bf16),
            pltpu.VMEM((rows, width), bf16),
            pltpu.VMEM((rows, width), bf16),
            pltpu.VMEM((width, rows), bf16),
            pltpu.VMEM((rows, width), bf16),
            pltpu.VMEM((rows, 128), bf16),
            pltpu.VMEM((rows, 128), bf16),
            pltpu.VMEM((width, rows), f32),
            pltpu.VMEM((width // HEAD * rows, rows), f32),
            pltpu.VMEM((rows, 3 * width), bf16),
            pltpu.VMEM((rows, 128), f32),
            pltpu.VMEM((rows, width), f32),
            pltpu.VMEM((rows, width), f32),
            dma((n,)),
            dma((n,)),
            dma((n,)),
            dma((n,)),
            dma((n,)),
            dma((n,)),
            dma((2,)),
            dma((2,)),
            pltpu.SemaphoreType.REGULAR,
        ],
        compiler_params=pltpu.CompilerParams(
            collective_id=0, has_side_effects=True, vmem_limit_bytes=40 * 1024 * 1024
        ),
        name="patch_attention_grad",
    )(*operands)


def solution(mesh):
    return jax.shard_map(
        per_device,
        mesh=mesh,
        in_specs=(
            P("section", "seq", None),
            P("section", "seq", None),
            P("section", None, None),
            P("section", None, None),
            P("section", None),
            P("section", None),
            P("section", "seq", None),
            P("section", "seq", None),
            P("section", "seq", None),
        ),
        out_specs=P("section", "seq", None),
        check_vma=False,
    )
```

```python
import functools
import math

import jax
import jax.numpy as jnp
from jax import lax
from jax.experimental import pallas as pl
from jax.experimental.pallas import tpu as pltpu
from jax.sharding import PartitionSpec as P

HEAD = 16
MESH = pl.DeviceIdType.MESH
LAST = (((1,), (1,)), ((), ()))
GROUP = 4


def dot(a, b):
    return jnp.dot(a, b, preferred_element_type=jnp.float32)


def dot_nt(a, b):
    return lax.dot_general(a, b, LAST, preferred_element_type=jnp.float32)


def each(first, count, body):
    if count - first <= 8:
        for step in by_distance(first, count):
            body(step)
    else:
        lax.fori_loop(first, count, lambda step, carry: (body(step), carry)[1], 0)


def by_distance(first, count):
    return sorted(range(first, count), key=lambda step: (abs(step - count // 2), step))


def iota(shape, axis):
    return lax.broadcasted_iota(jnp.int32, shape, axis)


def kernel(
    n,
    sections,
    paired,
    x_hbm,
    up_hbm,
    w_hbm,
    wo_hbm,
    gain_hbm,
    bias_hbm,
    send_hbm,
    recv_hbm,
    len_hbm,
    out_ref,
    x_ref,
    up_ref,
    w_ref,
    wo_ref,
    gain_ref,
    bias_ref,
    send_ref,
    recv_ref,
    len_ref,
    load_sem,
    send_x,
    recv_x,
    send_o,
    recv_o,
    send_b,
    recv_b,
    up_next,
    order_own,
    order_next,
    xhat_ref,
    q_ref,
    k_ref,
    v_ref,
    kt_ref,
    do_ref,
    feat_q,
    feat_k,
    dqt_ref,
    probs_ref,
    dqkv_ref,
    inverse_ref,
    dk_ref,
    dv_ref,
    sx_sem,
    rx_sem,
    so_sem,
    ro_sem,
    sb_sem,
    rb_sem,
    up_sem,
    order_sem,
    turn_sem,
):
    me = lax.axis_index("seq")
    section = lax.axis_index("section")
    rows, wide = x_ref.shape[1], x_ref.shape[2]
    width = wo_ref.shape[1]
    slot = send_x.shape[1]
    block = rows // n
    half = 128

    def spread(values):
        if slot == block:
            return values.reshape(n, slot, values.shape[1])
        place = iota((n * slot, rows), 0)
        source = jnp.where(place % slot < block, place // slot * block + place % slot, -1)
        pick = (source == iota((n * slot, rows), 1)).astype(jnp.bfloat16)
        return dot(pick, values).astype(jnp.bfloat16).reshape(n, slot, values.shape[1])

    def gather(values):
        values = values.reshape(n * slot, values.shape[2])
        if slot == block:
            return values
        place = iota((rows, n * slot), 0)
        pick = (place // block * slot + place % block == iota((rows, n * slot), 1)).astype(jnp.bfloat16)
        return dot(pick, values).astype(jnp.bfloat16)

    def x_copy(local, there, peer):
        return pltpu.make_async_remote_copy(
            send_x.at[local], recv_x.at[there], sx_sem.at[local], rx_sem.at[there],
            device_id=(peer, section), device_id_type=MESH,
        )

    def o_copy(local, there, peer):
        return pltpu.make_async_remote_copy(
            send_o.at[local], recv_o.at[there], so_sem.at[local], ro_sem.at[there],
            device_id=(peer, section), device_id_type=MESH,
        )

    def b_copy(local, there, peer):
        return pltpu.make_async_remote_copy(
            send_b.at[local], recv_b.at[there], sb_sem.at[local], rb_sem.at[there],
            device_id=(peer, section - 1), device_id_type=MESH,
        )

    def up_copy():
        return pltpu.make_async_remote_copy(
            up_ref.at[0], up_next, up_sem.at[0], up_sem.at[1],
            device_id=(me, section - 1), device_id_type=MESH,
        )

    def order_copy():
        return pltpu.make_async_remote_copy(
            order_own, order_next, order_sem.at[0], order_sem.at[1],
            device_id=(me, section - 1), device_id_type=MESH,
        )

    def x_sent(step):
        peer = lax.rem(me + step, n)
        x_copy(peer, me, peer).wait_send()

    far = by_distance(1, n)[:5] if paired else []
    loads = [
        pltpu.make_async_copy(source, target, load_sem.at[i])
        for i, (source, target) in enumerate(
            [
                (x_hbm, x_ref),
                (up_hbm, up_ref),
                (w_hbm, w_ref),
                (wo_hbm, wo_ref),
                (gain_hbm, gain_ref),
                (bias_hbm, bias_ref),
                (send_hbm, send_ref),
                (recv_hbm, recv_ref),
                (len_hbm, len_ref),
            ]
        )
    ]
    barrier = pltpu.get_barrier_semaphore()

    @pl.when(section > 0)
    def _():
        for i in (6, 0, 3, 1, 7, 8, 4, 5, 2):
            loads[i].start()

        def greet(step):
            pl.semaphore_signal(
                barrier, inc=1, device_id=(lax.rem(me + step, n), section), device_id_type=MESH
            )

        each(1, n, greet)

    @pl.when(section < sections - 1)
    def _():
        def greet(step):
            pl.semaphore_signal(
                barrier, inc=1, device_id=(lax.rem(me + step, n), section + 1), device_id_type=MESH
            )

        each(0, n, greet)

    first_of_pair = (section % 2 == 0) & (section > 0)
    second_of_pair = (section % 2 == 1) & (section > 1)
    if paired:

        @pl.when(second_of_pair)
        def _():
            pl.semaphore_signal(barrier, inc=1, device_id=(me, section - 1), device_id_type=MESH)

    @pl.when(section > 0)
    def _():
        loads[6].wait()
        order_own[...] = jnp.broadcast_to(send_ref[0], order_own.shape)
        row_of = send_ref[0].astype(jnp.float32)
        eye = iota((rows, rows), 0) == iota((rows, rows), 1)
        column = jnp.sum(jnp.where(eye, row_of, 0.0), axis=1, keepdims=True).astype(jnp.int32)
        pick = jnp.where(column == iota((rows, rows), 1), 1.0, 0.0).astype(jnp.bfloat16)
        loads[0].wait()
        send_x[...] = spread(dot(pick, x_ref[0]).astype(jnp.bfloat16))
        greetings = 2 * n - 1
        if paired:
            greetings = greetings + first_of_pair.astype(jnp.int32)
        pl.semaphore_wait(barrier, greetings)
        if paired:

            @pl.when(second_of_pair)
            def _():
                pl.semaphore_wait(turn_sem, 1)

        each(1, n, lambda step: x_copy(lax.rem(me + step, n), me, lax.rem(me + step, n)).start())
        loads[1].wait()
        loads[3].wait()
        out_common = dot_nt(up_ref[0], wo_ref[0]).astype(jnp.bfloat16)
        send_o[...] = spread(dot(pick, out_common).astype(jnp.bfloat16))
        each(1, n, lambda step: o_copy(lax.rem(me + step, n), me, lax.rem(me + step, n)).start())
        up_copy().start()
        order_copy().start()
        recv_x[me] = send_x[me]
        recv_o[me] = send_o[me]

        loads[7].wait()
        loads[8].wait()
        place = iota((1, rows), 1)
        end = jnp.zeros((1, 1), jnp.int32)
        segment = jnp.zeros((1, rows), jnp.float32)
        for patch in range(len_ref.shape[2]):
            end = end + len_ref[0, :, patch : patch + 1]
            segment = segment + jnp.where(place >= end, 1.0, 0.0)
        at = recv_ref[0] == iota((rows, rows), 0)
        patch_of = jnp.sum(jnp.where(at, segment, 0.0), axis=1, keepdims=True).astype(jnp.int32)
        lanes = iota((rows, half), 1)
        feat_k[...] = jnp.where(patch_of == lanes, 1.0, 0.0).astype(jnp.bfloat16)
        feat_q[...] = jnp.where(patch_of == lanes, 0.0, -1e30).astype(jnp.bfloat16)

        for i in (4, 5, 2):
            loads[i].wait()

        if paired:

            @pl.when(first_of_pair)
            def _():
                for step in far:
                    x_sent(step)
                pl.semaphore_signal(turn_sem, inc=1, device_id=(me, section + 1), device_id_type=MESH)

        def x_wait(step):
            peer = lax.rem(me + step, n)
            x_copy(peer, peer, peer).wait_recv()

        each(1, n, x_wait)
        values = gather(recv_x[...]).astype(jnp.float32)
        centered = values - jnp.mean(values, axis=-1, keepdims=True)
        inverse = lax.rsqrt(jnp.mean(centered * centered, axis=-1, keepdims=True) + 1e-05)
        xhat = centered * inverse
        xhat_ref[...] = xhat
        inverse_ref[...] = jnp.broadcast_to(inverse, inverse_ref.shape)
        normed = (xhat * gain_ref[...] + bias_ref[...]).astype(jnp.bfloat16)
        q_ref[...] = dot(normed, w_ref[0, :, :width]).astype(jnp.bfloat16)
        key = dot(normed, w_ref[0, :, width : 2 * width]).astype(jnp.bfloat16)
        k_ref[...] = key
        kt_ref[...] = key.astype(jnp.float32).T.astype(jnp.bfloat16)
        v_ref[...] = dot(normed, w_ref[0, :, 2 * width :]).astype(jnp.bfloat16)

        rate = float(HEAD) ** (-0.5) * math.log2(math.e)
        lane_head = iota((rows, half), 1) // HEAD
        zero = jnp.zeros((rows, half), jnp.bfloat16)
        groups = half // HEAD // GROUP

        def softmax_heads(part, group):
            columns = slice(part * half, (part + 1) * half)
            query_right = jnp.concatenate([q_ref[:, columns], feat_q[...]], axis=1)
            mine = [lane_head == group * GROUP + i for i in range(GROUP)]
            key, feature = k_ref[:, columns], feat_k[...]
            keys = jnp.concatenate(
                [jnp.concatenate([jnp.where(m, key, zero), feature], axis=1) for m in mine], axis=0
            )
            scores = dot_nt(keys, query_right)
            for i in range(GROUP):
                start = pl.multiple_of(((part * groups + group) * GROUP + i) * rows, rows)
                for first in range(0, rows, half):
                    some = slice(first, first + half)
                    score = scores[i * rows : (i + 1) * rows, some]
                    expo = jnp.exp2((score - jnp.max(score, axis=0, keepdims=True)) * rate)
                    probs_ref[pl.ds(start, rows), some] = expo * (1.0 / jnp.sum(expo, axis=0, keepdims=True))

        def gradient_heads(part, group):
            columns = slice(part * half, (part + 1) * half)
            query, value, dout = q_ref[:, columns], v_ref[:, columns], do_ref[:, columns]
            mine = [lane_head == group * GROUP + i for i in range(GROUP)]
            values = jnp.concatenate([jnp.where(m, value, zero) for m in mine], axis=0)
            dprobs = dot_nt(values, dout)
            weights, dscores = [], []
            for i in range(GROUP):
                start = pl.multiple_of(((part * groups + group) * GROUP + i) * rows, rows)
                weight, dscore = [], []
                for first in range(0, rows, half):
                    some = slice(first, first + half)
                    probs = probs_ref[pl.ds(start, rows), some]
                    dprob = dprobs[i * rows : (i + 1) * rows, some]
                    inner = jnp.sum(dprob * probs, axis=0, keepdims=True)
                    weight.append(probs.astype(jnp.bfloat16))
                    dscore.append((probs * (dprob - inner)).astype(jnp.bfloat16))
                weights.append(jnp.concatenate(weight, axis=1))
                dscores.append(jnp.concatenate(dscore, axis=1))
            dkeys = dot(jnp.concatenate(dscores, axis=0), query)
            dvalues = dot(jnp.concatenate(weights, axis=0), dout)
            dkey, dvalue = dk_ref[:, columns], dv_ref[:, columns]
            for i in range(GROUP):
                dkey = jnp.where(mine[i], dkeys[i * rows : (i + 1) * rows], dkey)
                dvalue = jnp.where(mine[i], dvalues[i * rows : (i + 1) * rows], dvalue)
                start = pl.multiple_of(part * half + (group * GROUP + i) * HEAD, HEAD)
                dqt_ref[pl.ds(start, HEAD), :] = dot(kt_ref[pl.ds(start, HEAD), :], dscores[i])
            dk_ref[:, columns] = dkey
            dv_ref[:, columns] = dvalue

        def all_heads(some_heads):
            for part in range(width // half):
                lax.fori_loop(0, groups, lambda group, carry: (some_heads(part, group), carry)[1], 0)

        all_heads(softmax_heads)

        def o_wait(step):
            peer = lax.rem(me + step, n)
            o_copy(peer, peer, peer).wait_recv()

        each(1, n, o_wait)
        do_ref[...] = gather(recv_o[...])
        all_heads(gradient_heads)

        scale = float(HEAD) ** (-0.5)
        dqkv_ref[:, :width] = (dqt_ref[...].T * scale).astype(jnp.bfloat16)
        dqkv_ref[:, width : 2 * width] = (dk_ref[...] * scale).astype(jnp.bfloat16)
        dqkv_ref[:, 2 * width :] = dv_ref[...].astype(jnp.bfloat16)
        pieces = 2 if slot == block and n % 2 == 0 else 1
        peers, few = n // pieces, rows // pieces
        for piece in range(pieces):
            which = lax.rem(me // peers + 1 + piece, pieces)
            some = pl.ds(pl.multiple_of(which * few, few), few)
            grad = dot_nt(dqkv_ref[some, :], w_ref[0]) * gain_ref[...]
            xhat = xhat_ref[some, :]
            mean = jnp.mean(grad, axis=-1, keepdims=True)
            cross = jnp.mean(grad * xhat, axis=-1, keepdims=True)
            branch = (inverse_ref[some, :1] * (grad - mean - xhat * cross)).astype(jnp.bfloat16)
            if pieces == 1:
                send_b[...] = spread(branch)
            else:
                send_b[pl.ds(which * peers, peers)] = branch.reshape(peers, slot, wide)

            def send_back(step, which=which):
                peer = which * peers + lax.rem(me + step, peers)
                b_copy(peer, me, peer).start()

            each(0, peers, send_back)

    @pl.when(section < sections - 1)
    def _():
        order_copy().wait_recv()
        up_copy().wait_recv()
        pick = jnp.where(order_next[0:1, :] == iota((rows, rows), 0), 1.0, 0.0).astype(jnp.bfloat16)

        def b_wait(step):
            peer = lax.rem(me + step, n)
            b_copy(peer, peer, peer).wait_recv()

        each(0, n, b_wait)
        branch = dot(pick, gather(recv_b[...]))
        out_ref[0] = (up_next[...].astype(jnp.float32) + branch).astype(jnp.bfloat16)

    @pl.when(section == sections - 1)
    def _():
        out_ref[...] = jnp.zeros_like(out_ref)

    @pl.when(section > 0)
    def _():
        def sent(step):
            peer = lax.rem(me + step, n)
            o_copy(peer, me, peer).wait_send()
            if not paired or step not in far:
                x_sent(step)
            else:

                @pl.when(jnp.logical_not(first_of_pair))
                def _():
                    x_sent(step)

        each(1, n, sent)

        def sent_back(step):
            peer = lax.rem(me + step, n)
            b_copy(peer, me, peer).wait_send()

        each(0, n, sent_back)
        up_copy().wait_send()
        order_copy().wait_send()


def per_device(x, up, w_qkv, w_out, gain, bias, send_order, recv_order, lengths):
    n, sections = lax.axis_size("seq"), lax.axis_size("section")
    rows, wide = x.shape[1], x.shape[2]
    width = w_out.shape[1]
    slot = max(rows // n, 16)
    vmem = pl.BlockSpec(memory_space=pltpu.VMEM)
    bf16, f32 = jnp.bfloat16, jnp.float32
    dma = pltpu.SemaphoreType.DMA
    operands = (x, up, w_qkv, w_out, gain, bias, send_order, recv_order, lengths)
    operands = [pltpu.with_memory_space_constraint(a, pltpu.HBM) for a in operands]
    return pl.pallas_call(
        functools.partial(kernel, n, sections, sections % 2 == 0 and n <= 8),
        out_shape=jax.ShapeDtypeStruct(x.shape, bf16),
        in_specs=[pl.BlockSpec(memory_space=pltpu.HBM)] * 9,
        out_specs=vmem,
        scratch_shapes=[
            *[pltpu.VMEM(a.shape, a.dtype) for a in operands],
            dma((len(operands),)),
            pltpu.VMEM((n, slot, wide), bf16),
            pltpu.VMEM((n, slot, wide), bf16),
            pltpu.VMEM((n, slot, width), bf16),
            pltpu.VMEM((n, slot, width), bf16),
            pltpu.VMEM((n, slot, wide), bf16),
            pltpu.VMEM((n, slot, wide), bf16),
            pltpu.VMEM((rows, wide), bf16),
            pltpu.VMEM((8, rows), jnp.int32),
            pltpu.VMEM((8, rows), jnp.int32),
            pltpu.VMEM((rows, wide), f32),
            pltpu.VMEM((rows, width), bf16),
            pltpu.VMEM((rows, width), bf16),
            pltpu.VMEM((rows, width), bf16),
            pltpu.VMEM((width, rows), bf16),
            pltpu.VMEM((rows, width), bf16),
            pltpu.VMEM((rows, 128), bf16),
            pltpu.VMEM((rows, 128), bf16),
            pltpu.VMEM((width, rows), f32),
            pltpu.VMEM((width // HEAD * rows, rows), f32),
            pltpu.VMEM((rows, 3 * width), bf16),
            pltpu.VMEM((rows, 128), f32),
            pltpu.VMEM((rows, width), f32),
            pltpu.VMEM((rows, width), f32),
            dma((n,)),
            dma((n,)),
            dma((n,)),
            dma((n,)),
            dma((n,)),
            dma((n,)),
            dma((2,)),
            dma((2,)),
            pltpu.SemaphoreType.REGULAR,
        ],
        compiler_params=pltpu.CompilerParams(
            collective_id=0, has_side_effects=True, vmem_limit_bytes=40 * 1024 * 1024
        ),
        name="patch_attention_grad",
    )(*operands)


def solution(mesh):
    return jax.shard_map(
        per_device,
        mesh=mesh,
        in_specs=(
            P("section", "seq", None),
            P("section", "seq", None),
            P("section", None, None),
            P("section", None, None),
            P("section", None),
            P("section", None),
            P("section", "seq", None),
            P("section", "seq", None),
            P("section", "seq", None),
        ),
        out_specs=P("section", "seq", None),
        check_vma=False,
    )
```

```python
import functools
import math

import jax
import jax.numpy as jnp
from jax import lax
from jax.experimental import pallas as pl
from jax.experimental.pallas import tpu as pltpu
from jax.sharding import PartitionSpec as P

HEAD = 16
MESH = pl.DeviceIdType.MESH
LAST = (((1,), (1,)), ((), ()))
GROUP = 4


def dot(a, b):
    return jnp.dot(a, b, preferred_element_type=jnp.float32)


def dot_nt(a, b):
    return lax.dot_general(a, b, LAST, preferred_element_type=jnp.float32)


def each(first, count, body):
    if count - first <= 8:
        for step in by_distance(first, count):
            body(step)
    else:
        lax.fori_loop(first, count, lambda step, carry: (body(step), carry)[1], 0)


def by_distance(first, count):
    return sorted(range(first, count), key=lambda step: (abs(step - count // 2), step))


def iota(shape, axis):
    return lax.broadcasted_iota(jnp.int32, shape, axis)


def kernel(
    n,
    sections,
    paired,
    x_hbm,
    up_hbm,
    w_hbm,
    wo_hbm,
    gain_hbm,
    bias_hbm,
    send_hbm,
    recv_hbm,
    len_hbm,
    out_ref,
    x_ref,
    up_ref,
    w_ref,
    wo_ref,
    gain_ref,
    bias_ref,
    send_ref,
    recv_ref,
    len_ref,
    load_sem,
    send_x,
    recv_x,
    send_o,
    recv_o,
    send_b,
    recv_b,
    up_next,
    order_own,
    order_next,
    xhat_ref,
    q_ref,
    k_ref,
    v_ref,
    kt_ref,
    do_ref,
    feat_q,
    feat_k,
    dqt_ref,
    probs_ref,
    dqkv_ref,
    inverse_ref,
    dk_ref,
    dv_ref,
    sx_sem,
    rx_sem,
    so_sem,
    ro_sem,
    sb_sem,
    rb_sem,
    up_sem,
    order_sem,
    turn_sem,
):
    me = lax.axis_index("seq")
    section = lax.axis_index("section")
    rows, wide = x_ref.shape[1], x_ref.shape[2]
    width = wo_ref.shape[1]
    slot = send_x.shape[1]
    block = rows // n
    half = 128

    def spread(values):
        if slot == block:
            return values.reshape(n, slot, values.shape[1])
        place = iota((n * slot, rows), 0)
        source = jnp.where(place % slot < block, place // slot * block + place % slot, -1)
        pick = (source == iota((n * slot, rows), 1)).astype(jnp.bfloat16)
        return dot(pick, values).astype(jnp.bfloat16).reshape(n, slot, values.shape[1])

    def gather(values):
        values = values.reshape(n * slot, values.shape[2])
        if slot == block:
            return values
        place = iota((rows, n * slot), 0)
        pick = (place // block * slot + place % block == iota((rows, n * slot), 1)).astype(jnp.bfloat16)
        return dot(pick, values).astype(jnp.bfloat16)

    def x_copy(local, there, peer):
        return pltpu.make_async_remote_copy(
            send_x.at[local], recv_x.at[there], sx_sem.at[local], rx_sem.at[there],
            device_id=(peer, section), device_id_type=MESH,
        )

    def o_copy(local, there, peer):
        return pltpu.make_async_remote_copy(
            send_o.at[local], recv_o.at[there], so_sem.at[local], ro_sem.at[there],
            device_id=(peer, section), device_id_type=MESH,
        )

    def b_copy(local, there, peer):
        return pltpu.make_async_remote_copy(
            send_b.at[local], recv_b.at[there], sb_sem.at[local], rb_sem.at[there],
            device_id=(peer, section - 1), device_id_type=MESH,
        )

    def up_copy():
        return pltpu.make_async_remote_copy(
            up_ref.at[0], up_next, up_sem.at[0], up_sem.at[1],
            device_id=(me, section - 1), device_id_type=MESH,
        )

    def order_copy():
        return pltpu.make_async_remote_copy(
            order_own, order_next, order_sem.at[0], order_sem.at[1],
            device_id=(me, section - 1), device_id_type=MESH,
        )

    def x_sent(step):
        peer = lax.rem(me + step, n)
        x_copy(peer, me, peer).wait_send()

    far = by_distance(1, n)[:3] if paired else []
    loads = [
        pltpu.make_async_copy(source, target, load_sem.at[i])
        for i, (source, target) in enumerate(
            [
                (x_hbm, x_ref),
                (up_hbm, up_ref),
                (w_hbm, w_ref),
                (wo_hbm, wo_ref),
                (gain_hbm, gain_ref),
                (bias_hbm, bias_ref),
                (send_hbm, send_ref),
                (recv_hbm, recv_ref),
                (len_hbm, len_ref),
            ]
        )
    ]
    barrier = pltpu.get_barrier_semaphore()

    @pl.when(section > 0)
    def _():
        for i in (6, 0, 3, 1, 7, 8, 4, 5, 2):
            loads[i].start()

        def greet(step):
            pl.semaphore_signal(
                barrier, inc=1, device_id=(lax.rem(me + step, n), section), device_id_type=MESH
            )

        each(1, n, greet)

    @pl.when(section < sections - 1)
    def _():
        def greet(step):
            pl.semaphore_signal(
                barrier, inc=1, device_id=(lax.rem(me + step, n), section + 1), device_id_type=MESH
            )

        each(0, n, greet)

    first_of_pair = (section % 2 == 0) & (section > 0)
    second_of_pair = (section % 2 == 1) & (section > 1)
    if paired:

        @pl.when(second_of_pair)
        def _():
            pl.semaphore_signal(barrier, inc=1, device_id=(me, section - 1), device_id_type=MESH)

    @pl.when(section > 0)
    def _():
        loads[6].wait()
        order_own[...] = jnp.broadcast_to(send_ref[0], order_own.shape)
        row_of = send_ref[0].astype(jnp.float32)
        eye = iota((rows, rows), 0) == iota((rows, rows), 1)
        column = jnp.sum(jnp.where(eye, row_of, 0.0), axis=1, keepdims=True).astype(jnp.int32)
        pick = jnp.where(column == iota((rows, rows), 1), 1.0, 0.0).astype(jnp.bfloat16)
        loads[0].wait()
        send_x[...] = spread(dot(pick, x_ref[0]).astype(jnp.bfloat16))
        greetings = 2 * n - 1
        if paired:
            greetings = greetings + first_of_pair.astype(jnp.int32)
        pl.semaphore_wait(barrier, greetings)
        if paired:

            @pl.when(second_of_pair)
            def _():
                pl.semaphore_wait(turn_sem, 1)

        each(1, n, lambda step: x_copy(lax.rem(me + step, n), me, lax.rem(me + step, n)).start())
        loads[1].wait()
        loads[3].wait()
        out_common = dot_nt(up_ref[0], wo_ref[0]).astype(jnp.bfloat16)
        send_o[...] = spread(dot(pick, out_common).astype(jnp.bfloat16))
        each(1, n, lambda step: o_copy(lax.rem(me + step, n), me, lax.rem(me + step, n)).start())
        up_copy().start()
        order_copy().start()
        recv_x[me] = send_x[me]
        recv_o[me] = send_o[me]

        loads[7].wait()
        loads[8].wait()
        place = iota((1, rows), 1)
        end = jnp.zeros((1, 1), jnp.int32)
        segment = jnp.zeros((1, rows), jnp.float32)
        for patch in range(len_ref.shape[2]):
            end = end + len_ref[0, :, patch : patch + 1]
            segment = segment + jnp.where(place >= end, 1.0, 0.0)
        at = recv_ref[0] == iota((rows, rows), 0)
        patch_of = jnp.sum(jnp.where(at, segment, 0.0), axis=1, keepdims=True).astype(jnp.int32)
        lanes = iota((rows, half), 1)
        feat_k[...] = jnp.where(patch_of == lanes, 1.0, 0.0).astype(jnp.bfloat16)
        feat_q[...] = jnp.where(patch_of == lanes, 0.0, -1e30).astype(jnp.bfloat16)

        for i in (4, 5, 2):
            loads[i].wait()

        if paired:

            @pl.when(first_of_pair)
            def _():
                for step in far:
                    x_sent(step)
                pl.semaphore_signal(turn_sem, inc=1, device_id=(me, section + 1), device_id_type=MESH)

        def x_wait(step):
            peer = lax.rem(me + step, n)
            x_copy(peer, peer, peer).wait_recv()

        each(1, n, x_wait)
        values = gather(recv_x[...]).astype(jnp.float32)
        centered = values - jnp.mean(values, axis=-1, keepdims=True)
        inverse = lax.rsqrt(jnp.mean(centered * centered, axis=-1, keepdims=True) + 1e-05)
        xhat = centered * inverse
        xhat_ref[...] = xhat
        inverse_ref[...] = jnp.broadcast_to(inverse, inverse_ref.shape)
        normed = (xhat * gain_ref[...] + bias_ref[...]).astype(jnp.bfloat16)
        q_ref[...] = dot(normed, w_ref[0, :, :width]).astype(jnp.bfloat16)
        key = dot(normed, w_ref[0, :, width : 2 * width]).astype(jnp.bfloat16)
        k_ref[...] = key
        kt_ref[...] = key.astype(jnp.float32).T.astype(jnp.bfloat16)
        v_ref[...] = dot(normed, w_ref[0, :, 2 * width :]).astype(jnp.bfloat16)

        rate = float(HEAD) ** (-0.5) * math.log2(math.e)
        lane_head = iota((rows, half), 1) // HEAD
        zero = jnp.zeros((rows, half), jnp.bfloat16)
        groups = half // HEAD // GROUP

        def softmax_heads(part, group):
            columns = slice(part * half, (part + 1) * half)
            query_right = jnp.concatenate([q_ref[:, columns], feat_q[...]], axis=1)
            mine = [lane_head == group * GROUP + i for i in range(GROUP)]
            key, feature = k_ref[:, columns], feat_k[...]
            keys = jnp.concatenate(
                [jnp.concatenate([jnp.where(m, key, zero), feature], axis=1) for m in mine], axis=0
            )
            scores = dot_nt(keys, query_right)
            for i in range(GROUP):
                start = ((part * groups + group) * GROUP + i) * rows
                for first in range(0, rows, half):
                    some = slice(first, first + half)
                    score = scores[i * rows : (i + 1) * rows, some]
                    expo = jnp.exp2((score - jnp.max(score, axis=0, keepdims=True)) * rate)
                    probs_ref[pl.ds(start, rows), some] = expo * (1.0 / jnp.sum(expo, axis=0, keepdims=True))

        def gradient_heads(part, group):
            columns = slice(part * half, (part + 1) * half)
            query, value, dout = q_ref[:, columns], v_ref[:, columns], do_ref[:, columns]
            mine = [lane_head == group * GROUP + i for i in range(GROUP)]
            values = jnp.concatenate([jnp.where(m, value, zero) for m in mine], axis=0)
            dprobs = dot_nt(values, dout)
            weights, dscores = [], []
            for i in range(GROUP):
                start = ((part * groups + group) * GROUP + i) * rows
                weight, dscore = [], []
                for first in range(0, rows, half):
                    some = slice(first, first + half)
                    probs = probs_ref[pl.ds(start, rows), some]
                    dprob = dprobs[i * rows : (i + 1) * rows, some]
                    inner = jnp.sum(dprob * probs, axis=0, keepdims=True)
                    weight.append(probs.astype(jnp.bfloat16))
                    dscore.append((probs * (dprob - inner)).astype(jnp.bfloat16))
                weights.append(jnp.concatenate(weight, axis=1))
                dscores.append(jnp.concatenate(dscore, axis=1))
            dkeys = dot(jnp.concatenate(dscores, axis=0), query)
            dvalues = dot(jnp.concatenate(weights, axis=0), dout)
            dkey, dvalue = dk_ref[:, columns], dv_ref[:, columns]
            for i in range(GROUP):
                dkey = jnp.where(mine[i], dkeys[i * rows : (i + 1) * rows], dkey)
                dvalue = jnp.where(mine[i], dvalues[i * rows : (i + 1) * rows], dvalue)
                start = part * half + (group * GROUP + i) * HEAD
                dqt_ref[pl.ds(start, HEAD), :] = dot(kt_ref[pl.ds(start, HEAD), :], dscores[i])
            dk_ref[:, columns] = dkey
            dv_ref[:, columns] = dvalue

        def all_heads(some_heads):
            for part in range(width // half):
                for group in range(groups):
                    some_heads(part, group)

        all_heads(softmax_heads)

        def o_wait(step):
            peer = lax.rem(me + step, n)
            o_copy(peer, peer, peer).wait_recv()

        each(1, n, o_wait)
        do_ref[...] = gather(recv_o[...])
        all_heads(gradient_heads)

        scale = float(HEAD) ** (-0.5)
        dqkv_ref[:, :width] = (dqt_ref[...].T * scale).astype(jnp.bfloat16)
        dqkv_ref[:, width : 2 * width] = (dk_ref[...] * scale).astype(jnp.bfloat16)
        dqkv_ref[:, 2 * width :] = dv_ref[...].astype(jnp.bfloat16)
        pieces = 2 if slot == block and n % 2 == 0 else 1
        peers, few = n // pieces, rows // pieces
        for piece in range(pieces):
            which = lax.rem(me // peers + 1 + piece, pieces)
            some = pl.ds(pl.multiple_of(which * few, few), few)
            grad = dot_nt(dqkv_ref[some, :], w_ref[0]) * gain_ref[...]
            xhat = xhat_ref[some, :]
            mean = jnp.mean(grad, axis=-1, keepdims=True)
            cross = jnp.mean(grad * xhat, axis=-1, keepdims=True)
            branch = (inverse_ref[some, :1] * (grad - mean - xhat * cross)).astype(jnp.bfloat16)
            if pieces == 1:
                send_b[...] = spread(branch)
            else:
                send_b[pl.ds(which * peers, peers)] = branch.reshape(peers, slot, wide)

            def send_back(step, which=which):
                peer = which * peers + lax.rem(me + step, peers)
                b_copy(peer, me, peer).start()

            each(0, peers, send_back)

    @pl.when(section < sections - 1)
    def _():
        order_copy().wait_recv()
        up_copy().wait_recv()
        pick = jnp.where(order_next[0:1, :] == iota((rows, rows), 0), 1.0, 0.0).astype(jnp.bfloat16)

        def b_wait(step):
            peer = lax.rem(me + step, n)
            b_copy(peer, peer, peer).wait_recv()

        each(0, n, b_wait)
        branch = dot(pick, gather(recv_b[...]))
        out_ref[0] = (up_next[...].astype(jnp.float32) + branch).astype(jnp.bfloat16)

    @pl.when(section == sections - 1)
    def _():
        out_ref[...] = jnp.zeros_like(out_ref)

    @pl.when(section > 0)
    def _():
        def sent(step):
            peer = lax.rem(me + step, n)
            o_copy(peer, me, peer).wait_send()
            if not paired or step not in far:
                x_sent(step)
            else:

                @pl.when(jnp.logical_not(first_of_pair))
                def _():
                    x_sent(step)

        each(1, n, sent)

        def sent_back(step):
            peer = lax.rem(me + step, n)
            b_copy(peer, me, peer).wait_send()

        each(0, n, sent_back)
        up_copy().wait_send()
        order_copy().wait_send()


def per_device(x, up, w_qkv, w_out, gain, bias, send_order, recv_order, lengths):
    n, sections = lax.axis_size("seq"), lax.axis_size("section")
    rows, wide = x.shape[1], x.shape[2]
    width = w_out.shape[1]
    slot = max(rows // n, 16)
    vmem = pl.BlockSpec(memory_space=pltpu.VMEM)
    bf16, f32 = jnp.bfloat16, jnp.float32
    dma = pltpu.SemaphoreType.DMA
    operands = (x, up, w_qkv, w_out, gain, bias, send_order, recv_order, lengths)
    operands = [pltpu.with_memory_space_constraint(a, pltpu.HBM) for a in operands]
    return pl.pallas_call(
        functools.partial(kernel, n, sections, sections % 2 == 0 and n <= 8),
        out_shape=jax.ShapeDtypeStruct(x.shape, bf16),
        in_specs=[pl.BlockSpec(memory_space=pltpu.HBM)] * 9,
        out_specs=vmem,
        scratch_shapes=[
            *[pltpu.VMEM(a.shape, a.dtype) for a in operands],
            dma((len(operands),)),
            pltpu.VMEM((n, slot, wide), bf16),
            pltpu.VMEM((n, slot, wide), bf16),
            pltpu.VMEM((n, slot, width), bf16),
            pltpu.VMEM((n, slot, width), bf16),
            pltpu.VMEM((n, slot, wide), bf16),
            pltpu.VMEM((n, slot, wide), bf16),
            pltpu.VMEM((rows, wide), bf16),
            pltpu.VMEM((8, rows), jnp.int32),
            pltpu.VMEM((8, rows), jnp.int32),
            pltpu.VMEM((rows, wide), f32),
            pltpu.VMEM((rows, width), bf16),
            pltpu.VMEM((rows, width), bf16),
            pltpu.VMEM((rows, width), bf16),
            pltpu.VMEM((width, rows), bf16),
            pltpu.VMEM((rows, width), bf16),
            pltpu.VMEM((rows, 128), bf16),
            pltpu.VMEM((rows, 128), bf16),
            pltpu.VMEM((width, rows), f32),
            pltpu.VMEM((width // HEAD * rows, rows), f32),
            pltpu.VMEM((rows, 3 * width), bf16),
            pltpu.VMEM((rows, 128), f32),
            pltpu.VMEM((rows, width), f32),
            pltpu.VMEM((rows, width), f32),
            dma((n,)),
            dma((n,)),
            dma((n,)),
            dma((n,)),
            dma((n,)),
            dma((n,)),
            dma((2,)),
            dma((2,)),
            pltpu.SemaphoreType.REGULAR,
        ],
        compiler_params=pltpu.CompilerParams(
            collective_id=0, has_side_effects=True, vmem_limit_bytes=40 * 1024 * 1024
        ),
        name="patch_attention_grad",
    )(*operands)


def solution(mesh):
    return jax.shard_map(
        per_device,
        mesh=mesh,
        in_specs=(
            P("section", "seq", None),
            P("section", "seq", None),
            P("section", None, None),
            P("section", None, None),
            P("section", None),
            P("section", None),
            P("section", "seq", None),
            P("section", "seq", None),
            P("section", "seq", None),
        ),
        out_specs=P("section", "seq", None),
        check_vma=False,
    )
```

```python
import functools
import math

import jax
import jax.numpy as jnp
from jax import lax
from jax.experimental import pallas as pl
from jax.experimental.pallas import tpu as pltpu
from jax.sharding import PartitionSpec as P

HEAD = 16
MESH = pl.DeviceIdType.MESH
LAST = (((1,), (1,)), ((), ()))
GROUP = 4


def dot(a, b):
    return jnp.dot(a, b, preferred_element_type=jnp.float32)


def dot_nt(a, b):
    return lax.dot_general(a, b, LAST, preferred_element_type=jnp.float32)


def each(first, count, body):
    if count - first <= 8:
        for step in by_distance(first, count):
            body(step)
    else:
        lax.fori_loop(first, count, lambda step, carry: (body(step), carry)[1], 0)


def by_distance(first, count):
    return sorted(range(first, count), key=lambda step: (abs(step - count // 2), step))


def iota(shape, axis):
    return lax.broadcasted_iota(jnp.int32, shape, axis)


def kernel(
    n,
    sections,
    paired,
    x_hbm,
    up_hbm,
    w_hbm,
    wo_hbm,
    gain_hbm,
    bias_hbm,
    send_hbm,
    recv_hbm,
    len_hbm,
    out_ref,
    x_ref,
    up_ref,
    w_ref,
    wo_ref,
    gain_ref,
    bias_ref,
    send_ref,
    recv_ref,
    len_ref,
    load_sem,
    send_x,
    recv_x,
    send_o,
    recv_o,
    send_b,
    recv_b,
    up_next,
    order_own,
    order_next,
    xhat_ref,
    q_ref,
    k_ref,
    v_ref,
    kt_ref,
    do_ref,
    feat_q,
    feat_k,
    dqt_ref,
    probs_ref,
    dqkv_ref,
    inverse_ref,
    dk_ref,
    dv_ref,
    sx_sem,
    rx_sem,
    so_sem,
    ro_sem,
    sb_sem,
    rb_sem,
    up_sem,
    order_sem,
    turn_sem,
):
    me = lax.axis_index("seq")
    section = lax.axis_index("section")
    rows, wide = x_ref.shape[1], x_ref.shape[2]
    width = wo_ref.shape[1]
    slot = send_x.shape[1]
    block = rows // n
    half = 128

    def spread(values):
        if slot == block:
            return values.reshape(n, slot, values.shape[1])
        place = iota((n * slot, rows), 0)
        source = jnp.where(place % slot < block, place // slot * block + place % slot, -1)
        pick = (source == iota((n * slot, rows), 1)).astype(jnp.bfloat16)
        return dot(pick, values).astype(jnp.bfloat16).reshape(n, slot, values.shape[1])

    def gather(values):
        values = values.reshape(n * slot, values.shape[2])
        if slot == block:
            return values
        place = iota((rows, n * slot), 0)
        pick = (place // block * slot + place % block == iota((rows, n * slot), 1)).astype(jnp.bfloat16)
        return dot(pick, values).astype(jnp.bfloat16)

    def x_copy(local, there, peer):
        return pltpu.make_async_remote_copy(
            send_x.at[local], recv_x.at[there], sx_sem.at[local], rx_sem.at[there],
            device_id=(peer, section), device_id_type=MESH,
        )

    def o_copy(local, there, peer):
        return pltpu.make_async_remote_copy(
            send_o.at[local], recv_o.at[there], so_sem.at[local], ro_sem.at[there],
            device_id=(peer, section), device_id_type=MESH,
        )

    def b_copy(local, there, peer):
        return pltpu.make_async_remote_copy(
            send_b.at[local], recv_b.at[there], sb_sem.at[local], rb_sem.at[there],
            device_id=(peer, section - 1), device_id_type=MESH,
        )

    def up_copy():
        return pltpu.make_async_remote_copy(
            up_ref.at[0], up_next, up_sem.at[0], up_sem.at[1],
            device_id=(me, section - 1), device_id_type=MESH,
        )

    def order_copy():
        return pltpu.make_async_remote_copy(
            order_own, order_next, order_sem.at[0], order_sem.at[1],
            device_id=(me, section - 1), device_id_type=MESH,
        )

    def x_sent(step):
        peer = lax.rem(me + step, n)
        x_copy(peer, me, peer).wait_send()

    far = by_distance(1, n)[:5] if paired else []
    loads = [
        pltpu.make_async_copy(source, target, load_sem.at[i])
        for i, (source, target) in enumerate(
            [
                (x_hbm, x_ref),
                (up_hbm, up_ref),
                (w_hbm, w_ref),
                (wo_hbm, wo_ref),
                (gain_hbm, gain_ref),
                (bias_hbm, bias_ref),
                (send_hbm, send_ref),
                (recv_hbm, recv_ref),
                (len_hbm, len_ref),
            ]
        )
    ]
    barrier = pltpu.get_barrier_semaphore()

    @pl.when(section > 0)
    def _():
        for i in (6, 0, 3, 1, 7, 8, 4, 5, 2):
            loads[i].start()

        def greet(step):
            pl.semaphore_signal(
                barrier, inc=1, device_id=(lax.rem(me + step, n), section), device_id_type=MESH
            )

        each(1, n, greet)

    @pl.when(section < sections - 1)
    def _():
        def greet(step):
            pl.semaphore_signal(
                barrier, inc=1, device_id=(lax.rem(me + step, n), section + 1), device_id_type=MESH
            )

        each(0, n, greet)

    first_of_pair = (section % 2 == 0) & (section > 0)
    second_of_pair = (section % 2 == 1) & (section > 1)
    if paired:

        @pl.when(second_of_pair)
        def _():
            pl.semaphore_signal(barrier, inc=1, device_id=(me, section - 1), device_id_type=MESH)

    @pl.when(section > 0)
    def _():
        loads[6].wait()
        order_own[...] = jnp.broadcast_to(send_ref[0], order_own.shape)
        row_of = send_ref[0].astype(jnp.float32)
        eye = iota((rows, rows), 0) == iota((rows, rows), 1)
        column = jnp.sum(jnp.where(eye, row_of, 0.0), axis=1, keepdims=True).astype(jnp.int32)
        pick = jnp.where(column == iota((rows, rows), 1), 1.0, 0.0).astype(jnp.bfloat16)
        loads[0].wait()
        send_x[...] = spread(dot(pick, x_ref[0]).astype(jnp.bfloat16))
        greetings = 2 * n - 1
        if paired:
            greetings = greetings + first_of_pair.astype(jnp.int32)
        pl.semaphore_wait(barrier, greetings)
        if paired:

            @pl.when(second_of_pair)
            def _():
                pl.semaphore_wait(turn_sem, 1)

        each(1, n, lambda step: x_copy(lax.rem(me + step, n), me, lax.rem(me + step, n)).start())
        loads[1].wait()
        loads[3].wait()
        out_common = dot_nt(up_ref[0], wo_ref[0]).astype(jnp.bfloat16)
        send_o[...] = spread(dot(pick, out_common).astype(jnp.bfloat16))
        each(1, n, lambda step: o_copy(lax.rem(me + step, n), me, lax.rem(me + step, n)).start())
        up_copy().start()
        order_copy().start()
        recv_x[me] = send_x[me]
        recv_o[me] = send_o[me]

        loads[7].wait()
        loads[8].wait()
        place = iota((1, rows), 1)
        end = jnp.zeros((1, 1), jnp.int32)
        segment = jnp.zeros((1, rows), jnp.float32)
        for patch in range(len_ref.shape[2]):
            end = end + len_ref[0, :, patch : patch + 1]
            segment = segment + jnp.where(place >= end, 1.0, 0.0)
        at = recv_ref[0] == iota((rows, rows), 0)
        patch_of = jnp.sum(jnp.where(at, segment, 0.0), axis=1, keepdims=True).astype(jnp.int32)
        lanes = iota((rows, half), 1)
        feat_k[...] = jnp.where(patch_of == lanes, 1.0, 0.0).astype(jnp.bfloat16)
        feat_q[...] = jnp.where(patch_of == lanes, 0.0, -1e30).astype(jnp.bfloat16)

        for i in (4, 5, 2):
            loads[i].wait()

        if paired:

            @pl.when(first_of_pair)
            def _():
                for step in far:
                    x_sent(step)
                pl.semaphore_signal(turn_sem, inc=1, device_id=(me, section + 1), device_id_type=MESH)

        def x_wait(step):
            peer = lax.rem(me + step, n)
            x_copy(peer, peer, peer).wait_recv()

        each(1, n, x_wait)
        values = gather(recv_x[...]).astype(jnp.float32)
        centered = values - jnp.mean(values, axis=-1, keepdims=True)
        inverse = lax.rsqrt(jnp.mean(centered * centered, axis=-1, keepdims=True) + 1e-05)
        xhat = centered * inverse
        xhat_ref[...] = xhat
        inverse_ref[...] = jnp.broadcast_to(inverse, inverse_ref.shape)
        normed = (xhat * gain_ref[...] + bias_ref[...]).astype(jnp.bfloat16)
        q_ref[...] = dot(normed, w_ref[0, :, :width]).astype(jnp.bfloat16)
        key = dot(normed, w_ref[0, :, width : 2 * width]).astype(jnp.bfloat16)
        k_ref[...] = key
        kt_ref[...] = key.astype(jnp.float32).T.astype(jnp.bfloat16)
        v_ref[...] = dot(normed, w_ref[0, :, 2 * width :]).astype(jnp.bfloat16)

        rate = float(HEAD) ** (-0.5) * math.log2(math.e)
        lane_head = iota((rows, half), 1) // HEAD
        zero = jnp.zeros((rows, half), jnp.bfloat16)
        groups = half // HEAD // GROUP

        def softmax_heads(part, group):
            columns = slice(part * half, (part + 1) * half)
            query_right = jnp.concatenate([q_ref[:, columns], feat_q[...]], axis=1)
            mine = [lane_head == group * GROUP + i for i in range(GROUP)]
            key, feature = k_ref[:, columns], feat_k[...]
            keys = jnp.concatenate(
                [jnp.concatenate([jnp.where(m, key, zero), feature], axis=1) for m in mine], axis=0
            )
            scores = dot_nt(keys, query_right)
            for i in range(GROUP):
                start = ((part * groups + group) * GROUP + i) * rows
                for first in range(0, rows, half):
                    some = slice(first, first + half)
                    score = scores[i * rows : (i + 1) * rows, some]
                    expo = jnp.exp2((score - jnp.max(score, axis=0, keepdims=True)) * rate)
                    probs_ref[pl.ds(start, rows), some] = expo * (1.0 / jnp.sum(expo, axis=0, keepdims=True))

        def gradient_heads(part, group):
            columns = slice(part * half, (part + 1) * half)
            query, value, dout = q_ref[:, columns], v_ref[:, columns], do_ref[:, columns]
            mine = [lane_head == group * GROUP + i for i in range(GROUP)]
            values = jnp.concatenate([jnp.where(m, value, zero) for m in mine], axis=0)
            dprobs = dot_nt(values, dout)
            weights, dscores = [], []
            for i in range(GROUP):
                start = ((part * groups + group) * GROUP + i) * rows
                weight, dscore = [], []
                for first in range(0, rows, half):
                    some = slice(first, first + half)
                    probs = probs_ref[pl.ds(start, rows), some]
                    dprob = dprobs[i * rows : (i + 1) * rows, some]
                    inner = jnp.sum(dprob * probs, axis=0, keepdims=True)
                    weight.append(probs.astype(jnp.bfloat16))
                    dscore.append((probs * (dprob - inner)).astype(jnp.bfloat16))
                weights.append(jnp.concatenate(weight, axis=1))
                dscores.append(jnp.concatenate(dscore, axis=1))
            dkeys = dot(jnp.concatenate(dscores, axis=0), query)
            dvalues = dot(jnp.concatenate(weights, axis=0), dout)
            dkey, dvalue = dk_ref[:, columns], dv_ref[:, columns]
            for i in range(GROUP):
                dkey = jnp.where(mine[i], dkeys[i * rows : (i + 1) * rows], dkey)
                dvalue = jnp.where(mine[i], dvalues[i * rows : (i + 1) * rows], dvalue)
                start = part * half + (group * GROUP + i) * HEAD
                dqt_ref[pl.ds(start, HEAD), :] = dot(kt_ref[pl.ds(start, HEAD), :], dscores[i])
            dk_ref[:, columns] = dkey
            dv_ref[:, columns] = dvalue

        def all_heads(some_heads):
            for part in range(width // half):
                for group in range(groups):
                    some_heads(part, group)

        all_heads(softmax_heads)

        def o_wait(step):
            peer = lax.rem(me + step, n)
            o_copy(peer, peer, peer).wait_recv()

        each(1, n, o_wait)
        do_ref[...] = gather(recv_o[...])
        all_heads(gradient_heads)

        scale = float(HEAD) ** (-0.5)
        dqkv_ref[:, :width] = (dqt_ref[...].T * scale).astype(jnp.bfloat16)
        dqkv_ref[:, width : 2 * width] = (dk_ref[...] * scale).astype(jnp.bfloat16)
        dqkv_ref[:, 2 * width :] = dv_ref[...].astype(jnp.bfloat16)
        pieces = 2 if slot == block and n % 2 == 0 else 1
        peers, few = n // pieces, rows // pieces
        for piece in range(pieces):
            which = lax.rem(me // peers + 1 + piece, pieces)
            some = pl.ds(pl.multiple_of(which * few, few), few)
            grad = dot_nt(dqkv_ref[some, :], w_ref[0]) * gain_ref[...]
            xhat = xhat_ref[some, :]
            mean = jnp.mean(grad, axis=-1, keepdims=True)
            cross = jnp.mean(grad * xhat, axis=-1, keepdims=True)
            branch = (inverse_ref[some, :1] * (grad - mean - xhat * cross)).astype(jnp.bfloat16)
            if pieces == 1:
                send_b[...] = spread(branch)
            else:
                send_b[pl.ds(which * peers, peers)] = branch.reshape(peers, slot, wide)

            def send_back(step, which=which):
                peer = which * peers + lax.rem(me + step, peers)
                b_copy(peer, me, peer).start()

            each(0, peers, send_back)

    @pl.when(section < sections - 1)
    def _():
        order_copy().wait_recv()
        up_copy().wait_recv()
        pick = jnp.where(order_next[0:1, :] == iota((rows, rows), 0), 1.0, 0.0).astype(jnp.bfloat16)

        def b_wait(step):
            peer = lax.rem(me + step, n)
            b_copy(peer, peer, peer).wait_recv()

        each(0, n, b_wait)
        branch = dot(pick, gather(recv_b[...]))
        out_ref[0] = (up_next[...].astype(jnp.float32) + branch).astype(jnp.bfloat16)

    @pl.when(section == sections - 1)
    def _():
        out_ref[...] = jnp.zeros_like(out_ref)

    @pl.when(section > 0)
    def _():
        def sent(step):
            peer = lax.rem(me + step, n)
            o_copy(peer, me, peer).wait_send()
            if not paired or step not in far:
                x_sent(step)
            else:

                @pl.when(jnp.logical_not(first_of_pair))
                def _():
                    x_sent(step)

        each(1, n, sent)

        def sent_back(step):
            peer = lax.rem(me + step, n)
            b_copy(peer, me, peer).wait_send()

        each(0, n, sent_back)
        up_copy().wait_send()
        order_copy().wait_send()


def per_device(x, up, w_qkv, w_out, gain, bias, send_order, recv_order, lengths):
    n, sections = lax.axis_size("seq"), lax.axis_size("section")
    rows, wide = x.shape[1], x.shape[2]
    width = w_out.shape[1]
    slot = max(rows // n, 16)
    vmem = pl.BlockSpec(memory_space=pltpu.VMEM)
    bf16, f32 = jnp.bfloat16, jnp.float32
    dma = pltpu.SemaphoreType.DMA
    operands = (x, up, w_qkv, w_out, gain, bias, send_order, recv_order, lengths)
    operands = [pltpu.with_memory_space_constraint(a, pltpu.HBM) for a in operands]
    return pl.pallas_call(
        functools.partial(kernel, n, sections, sections % 2 == 0 and n <= 8),
        out_shape=jax.ShapeDtypeStruct(x.shape, bf16),
        in_specs=[pl.BlockSpec(memory_space=pltpu.HBM)] * 9,
        out_specs=vmem,
        scratch_shapes=[
            *[pltpu.VMEM(a.shape, a.dtype) for a in operands],
            dma((len(operands),)),
            pltpu.VMEM((n, slot, wide), bf16),
            pltpu.VMEM((n, slot, wide), bf16),
            pltpu.VMEM((n, slot, width), bf16),
            pltpu.VMEM((n, slot, width), bf16),
            pltpu.VMEM((n, slot, wide), bf16),
            pltpu.VMEM((n, slot, wide), bf16),
            pltpu.VMEM((rows, wide), bf16),
            pltpu.VMEM((8, rows), jnp.int32),
            pltpu.VMEM((8, rows), jnp.int32),
            pltpu.VMEM((rows, wide), f32),
            pltpu.VMEM((rows, width), bf16),
            pltpu.VMEM((rows, width), bf16),
            pltpu.VMEM((rows, width), bf16),
            pltpu.VMEM((width, rows), bf16),
            pltpu.VMEM((rows, width), bf16),
            pltpu.VMEM((rows, 128), bf16),
            pltpu.VMEM((rows, 128), bf16),
            pltpu.VMEM((width, rows), f32),
            pltpu.VMEM((width // HEAD * rows, rows), f32),
            pltpu.VMEM((rows, 3 * width), bf16),
            pltpu.VMEM((rows, 128), f32),
            pltpu.VMEM((rows, width), f32),
            pltpu.VMEM((rows, width), f32),
            dma((n,)),
            dma((n,)),
            dma((n,)),
            dma((n,)),
            dma((n,)),
            dma((n,)),
            dma((2,)),
            dma((2,)),
            pltpu.SemaphoreType.REGULAR,
        ],
        compiler_params=pltpu.CompilerParams(
            collective_id=0, has_side_effects=True, vmem_limit_bytes=40 * 1024 * 1024
        ),
        name="patch_attention_grad",
    )(*operands)


def solution(mesh):
    return jax.shard_map(
        per_device,
        mesh=mesh,
        in_specs=(
            P("section", "seq", None),
            P("section", "seq", None),
            P("section", None, None),
            P("section", None, None),
            P("section", None),
            P("section", None),
            P("section", "seq", None),
            P("section", "seq", None),
            P("section", "seq", None),
        ),
        out_specs=P("section", "seq", None),
        check_vma=False,
    )
```

```python
import functools
import math

import jax
import jax.numpy as jnp
from jax import lax
from jax.experimental import pallas as pl
from jax.experimental.pallas import tpu as pltpu
from jax.sharding import PartitionSpec as P

HEAD = 16
MESH = pl.DeviceIdType.MESH
LAST = (((1,), (1,)), ((), ()))
GROUP = 8


def dot(a, b):
    return jnp.dot(a, b, preferred_element_type=jnp.float32)


def dot_nt(a, b):
    return lax.dot_general(a, b, LAST, preferred_element_type=jnp.float32)


def each(first, count, body):
    if count - first <= 8:
        for step in by_distance(first, count):
            body(step)
    else:
        lax.fori_loop(first, count, lambda step, carry: (body(step), carry)[1], 0)


def by_distance(first, count):
    return sorted(range(first, count), key=lambda step: (abs(step - count // 2), step))


def iota(shape, axis):
    return lax.broadcasted_iota(jnp.int32, shape, axis)


def kernel(
    n,
    sections,
    paired,
    x_hbm,
    up_hbm,
    w_hbm,
    wo_hbm,
    gain_hbm,
    bias_hbm,
    send_hbm,
    recv_hbm,
    len_hbm,
    out_ref,
    x_ref,
    up_ref,
    w_ref,
    wo_ref,
    gain_ref,
    bias_ref,
    send_ref,
    recv_ref,
    len_ref,
    load_sem,
    send_x,
    recv_x,
    send_o,
    recv_o,
    send_b,
    recv_b,
    up_next,
    order_own,
    order_next,
    xhat_ref,
    q_ref,
    k_ref,
    v_ref,
    kt_ref,
    do_ref,
    feat_q,
    feat_k,
    dqt_ref,
    probs_ref,
    dqkv_ref,
    inverse_ref,
    dk_ref,
    dv_ref,
    sx_sem,
    rx_sem,
    so_sem,
    ro_sem,
    sb_sem,
    rb_sem,
    up_sem,
    order_sem,
    turn_sem,
):
    me = lax.axis_index("seq")
    section = lax.axis_index("section")
    rows, wide = x_ref.shape[1], x_ref.shape[2]
    width = wo_ref.shape[1]
    slot = send_x.shape[1]
    block = rows // n
    half = 128

    def spread(values):
        if slot == block:
            return values.reshape(n, slot, values.shape[1])
        place = iota((n * slot, rows), 0)
        source = jnp.where(place % slot < block, place // slot * block + place % slot, -1)
        pick = (source == iota((n * slot, rows), 1)).astype(jnp.bfloat16)
        return dot(pick, values).astype(jnp.bfloat16).reshape(n, slot, values.shape[1])

    def gather(values):
        values = values.reshape(n * slot, values.shape[2])
        if slot == block:
            return values
        place = iota((rows, n * slot), 0)
        pick = (place // block * slot + place % block == iota((rows, n * slot), 1)).astype(jnp.bfloat16)
        return dot(pick, values).astype(jnp.bfloat16)

    def x_copy(local, there, peer):
        return pltpu.make_async_remote_copy(
            send_x.at[local], recv_x.at[there], sx_sem.at[local], rx_sem.at[there],
            device_id=(peer, section), device_id_type=MESH,
        )

    def o_copy(local, there, peer):
        return pltpu.make_async_remote_copy(
            send_o.at[local], recv_o.at[there], so_sem.at[local], ro_sem.at[there],
            device_id=(peer, section), device_id_type=MESH,
        )

    def b_copy(local, there, peer):
        return pltpu.make_async_remote_copy(
            send_b.at[local], recv_b.at[there], sb_sem.at[local], rb_sem.at[there],
            device_id=(peer, section - 1), device_id_type=MESH,
        )

    def up_copy():
        return pltpu.make_async_remote_copy(
            up_ref.at[0], up_next, up_sem.at[0], up_sem.at[1],
            device_id=(me, section - 1), device_id_type=MESH,
        )

    def order_copy():
        return pltpu.make_async_remote_copy(
            order_own, order_next, order_sem.at[0], order_sem.at[1],
            device_id=(me, section - 1), device_id_type=MESH,
        )

    def x_sent(step):
        peer = lax.rem(me + step, n)
        x_copy(peer, me, peer).wait_send()

    far = by_distance(1, n)[:5] if paired else []
    loads = [
        pltpu.make_async_copy(source, target, load_sem.at[i])
        for i, (source, target) in enumerate(
            [
                (x_hbm, x_ref),
                (up_hbm, up_ref),
                (w_hbm, w_ref),
                (wo_hbm, wo_ref),
                (gain_hbm, gain_ref),
                (bias_hbm, bias_ref),
                (send_hbm, send_ref),
                (recv_hbm, recv_ref),
                (len_hbm, len_ref),
            ]
        )
    ]
    barrier = pltpu.get_barrier_semaphore()

    @pl.when(section > 0)
    def _():
        for i in (6, 0, 3, 1, 7, 8, 4, 5, 2):
            loads[i].start()

        def greet(step):
            pl.semaphore_signal(
                barrier, inc=1, device_id=(lax.rem(me + step, n), section), device_id_type=MESH
            )

        each(1, n, greet)

    @pl.when(section < sections - 1)
    def _():
        def greet(step):
            pl.semaphore_signal(
                barrier, inc=1, device_id=(lax.rem(me + step, n), section + 1), device_id_type=MESH
            )

        each(0, n, greet)

    first_of_pair = (section % 2 == 0) & (section > 0)
    second_of_pair = (section % 2 == 1) & (section > 1)
    if paired:

        @pl.when(second_of_pair)
        def _():
            pl.semaphore_signal(barrier, inc=1, device_id=(me, section - 1), device_id_type=MESH)

    @pl.when(section > 0)
    def _():
        loads[6].wait()
        order_own[...] = jnp.broadcast_to(send_ref[0], order_own.shape)
        row_of = send_ref[0].astype(jnp.float32)
        eye = iota((rows, rows), 0) == iota((rows, rows), 1)
        column = jnp.sum(jnp.where(eye, row_of, 0.0), axis=1, keepdims=True).astype(jnp.int32)
        pick = jnp.where(column == iota((rows, rows), 1), 1.0, 0.0).astype(jnp.bfloat16)
        loads[0].wait()
        send_x[...] = spread(dot(pick, x_ref[0]).astype(jnp.bfloat16))
        greetings = 2 * n - 1
        if paired:
            greetings = greetings + first_of_pair.astype(jnp.int32)
        pl.semaphore_wait(barrier, greetings)
        if paired:

            @pl.when(second_of_pair)
            def _():
                pl.semaphore_wait(turn_sem, 1)

        each(1, n, lambda step: x_copy(lax.rem(me + step, n), me, lax.rem(me + step, n)).start())
        loads[1].wait()
        loads[3].wait()
        out_common = dot_nt(up_ref[0], wo_ref[0]).astype(jnp.bfloat16)
        send_o[...] = spread(dot(pick, out_common).astype(jnp.bfloat16))
        each(1, n, lambda step: o_copy(lax.rem(me + step, n), me, lax.rem(me + step, n)).start())
        up_copy().start()
        order_copy().start()
        recv_x[me] = send_x[me]
        recv_o[me] = send_o[me]

        loads[7].wait()
        loads[8].wait()
        place = iota((1, rows), 1)
        end = jnp.zeros((1, 1), jnp.int32)
        segment = jnp.zeros((1, rows), jnp.float32)
        for patch in range(len_ref.shape[2]):
            end = end + len_ref[0, :, patch : patch + 1]
            segment = segment + jnp.where(place >= end, 1.0, 0.0)
        at = recv_ref[0] == iota((rows, rows), 0)
        patch_of = jnp.sum(jnp.where(at, segment, 0.0), axis=1, keepdims=True).astype(jnp.int32)
        lanes = iota((rows, half), 1)
        feat_k[...] = jnp.where(patch_of == lanes, 1.0, 0.0).astype(jnp.bfloat16)
        feat_q[...] = jnp.where(patch_of == lanes, 0.0, -1e30).astype(jnp.bfloat16)

        for i in (4, 5, 2):
            loads[i].wait()

        if paired:

            @pl.when(first_of_pair)
            def _():
                for step in far:
                    x_sent(step)
                pl.semaphore_signal(turn_sem, inc=1, device_id=(me, section + 1), device_id_type=MESH)

        def x_wait(step):
            peer = lax.rem(me + step, n)
            x_copy(peer, peer, peer).wait_recv()

        each(1, n, x_wait)
        values = gather(recv_x[...]).astype(jnp.float32)
        centered = values - jnp.mean(values, axis=-1, keepdims=True)
        inverse = lax.rsqrt(jnp.mean(centered * centered, axis=-1, keepdims=True) + 1e-05)
        xhat = centered * inverse
        xhat_ref[...] = xhat
        inverse_ref[...] = jnp.broadcast_to(inverse, inverse_ref.shape)
        normed = (xhat * gain_ref[...] + bias_ref[...]).astype(jnp.bfloat16)
        q_ref[...] = dot(normed, w_ref[0, :, :width]).astype(jnp.bfloat16)
        key = dot(normed, w_ref[0, :, width : 2 * width]).astype(jnp.bfloat16)
        k_ref[...] = key
        kt_ref[...] = key.astype(jnp.float32).T.astype(jnp.bfloat16)
        v_ref[...] = dot(normed, w_ref[0, :, 2 * width :]).astype(jnp.bfloat16)

        rate = float(HEAD) ** (-0.5) * math.log2(math.e)
        lane_head = iota((rows, half), 1) // HEAD
        zero = jnp.zeros((rows, half), jnp.bfloat16)
        groups = half // HEAD // GROUP

        def softmax_heads(part, group):
            columns = slice(part * half, (part + 1) * half)
            query_right = jnp.concatenate([q_ref[:, columns], feat_q[...]], axis=1)
            mine = [lane_head == group * GROUP + i for i in range(GROUP)]
            key, feature = k_ref[:, columns], feat_k[...]
            keys = jnp.concatenate(
                [jnp.concatenate([jnp.where(m, key, zero), feature], axis=1) for m in mine], axis=0
            )
            scores = dot_nt(keys, query_right)
            for i in range(GROUP):
                start = ((part * groups + group) * GROUP + i) * rows
                for first in range(0, rows, half):
                    some = slice(first, first + half)
                    score = scores[i * rows : (i + 1) * rows, some]
                    expo = jnp.exp2((score - jnp.max(score, axis=0, keepdims=True)) * rate)
                    probs_ref[pl.ds(start, rows), some] = expo * (1.0 / jnp.sum(expo, axis=0, keepdims=True))

        def gradient_heads(part, group):
            columns = slice(part * half, (part + 1) * half)
            query, value, dout = q_ref[:, columns], v_ref[:, columns], do_ref[:, columns]
            mine = [lane_head == group * GROUP + i for i in range(GROUP)]
            values = jnp.concatenate([jnp.where(m, value, zero) for m in mine], axis=0)
            dprobs = dot_nt(values, dout)
            weights, dscores = [], []
            for i in range(GROUP):
                start = ((part * groups + group) * GROUP + i) * rows
                weight, dscore = [], []
                for first in range(0, rows, half):
                    some = slice(first, first + half)
                    probs = probs_ref[pl.ds(start, rows), some]
                    dprob = dprobs[i * rows : (i + 1) * rows, some]
                    inner = jnp.sum(dprob * probs, axis=0, keepdims=True)
                    weight.append(probs.astype(jnp.bfloat16))
                    dscore.append((probs * (dprob - inner)).astype(jnp.bfloat16))
                weights.append(jnp.concatenate(weight, axis=1))
                dscores.append(jnp.concatenate(dscore, axis=1))
            dkeys = dot(jnp.concatenate(dscores, axis=0), query)
            dvalues = dot(jnp.concatenate(weights, axis=0), dout)
            dkey, dvalue = dk_ref[:, columns], dv_ref[:, columns]
            for i in range(GROUP):
                dkey = jnp.where(mine[i], dkeys[i * rows : (i + 1) * rows], dkey)
                dvalue = jnp.where(mine[i], dvalues[i * rows : (i + 1) * rows], dvalue)
                start = part * half + (group * GROUP + i) * HEAD
                dqt_ref[pl.ds(start, HEAD), :] = dot(kt_ref[pl.ds(start, HEAD), :], dscores[i])
            dk_ref[:, columns] = dkey
            dv_ref[:, columns] = dvalue

        def all_heads(some_heads):
            for part in range(width // half):
                for group in range(groups):
                    some_heads(part, group)

        all_heads(softmax_heads)

        def o_wait(step):
            peer = lax.rem(me + step, n)
            o_copy(peer, peer, peer).wait_recv()

        each(1, n, o_wait)
        do_ref[...] = gather(recv_o[...])
        all_heads(gradient_heads)

        scale = float(HEAD) ** (-0.5)
        dqkv_ref[:, :width] = (dqt_ref[...].T * scale).astype(jnp.bfloat16)
        dqkv_ref[:, width : 2 * width] = (dk_ref[...] * scale).astype(jnp.bfloat16)
        dqkv_ref[:, 2 * width :] = dv_ref[...].astype(jnp.bfloat16)
        pieces = 2 if slot == block and n % 2 == 0 else 1
        peers, few = n // pieces, rows // pieces
        for piece in range(pieces):
            which = lax.rem(me // peers + 1 + piece, pieces)
            some = pl.ds(pl.multiple_of(which * few, few), few)
            grad = dot_nt(dqkv_ref[some, :], w_ref[0]) * gain_ref[...]
            xhat = xhat_ref[some, :]
            mean = jnp.mean(grad, axis=-1, keepdims=True)
            cross = jnp.mean(grad * xhat, axis=-1, keepdims=True)
            branch = (inverse_ref[some, :1] * (grad - mean - xhat * cross)).astype(jnp.bfloat16)
            if pieces == 1:
                send_b[...] = spread(branch)
            else:
                send_b[pl.ds(which * peers, peers)] = branch.reshape(peers, slot, wide)

            def send_back(step, which=which):
                peer = which * peers + lax.rem(me + step, peers)
                b_copy(peer, me, peer).start()

            each(0, peers, send_back)

    @pl.when(section < sections - 1)
    def _():
        order_copy().wait_recv()
        up_copy().wait_recv()
        pick = jnp.where(order_next[0:1, :] == iota((rows, rows), 0), 1.0, 0.0).astype(jnp.bfloat16)

        def b_wait(step):
            peer = lax.rem(me + step, n)
            b_copy(peer, peer, peer).wait_recv()

        each(0, n, b_wait)
        branch = dot(pick, gather(recv_b[...]))
        out_ref[0] = (up_next[...].astype(jnp.float32) + branch).astype(jnp.bfloat16)

    @pl.when(section == sections - 1)
    def _():
        out_ref[...] = jnp.zeros_like(out_ref)

    @pl.when(section > 0)
    def _():
        def sent(step):
            peer = lax.rem(me + step, n)
            o_copy(peer, me, peer).wait_send()
            if not paired or step not in far:
                x_sent(step)
            else:

                @pl.when(jnp.logical_not(first_of_pair))
                def _():
                    x_sent(step)

        each(1, n, sent)

        def sent_back(step):
            peer = lax.rem(me + step, n)
            b_copy(peer, me, peer).wait_send()

        each(0, n, sent_back)
        up_copy().wait_send()
        order_copy().wait_send()


def per_device(x, up, w_qkv, w_out, gain, bias, send_order, recv_order, lengths):
    n, sections = lax.axis_size("seq"), lax.axis_size("section")
    rows, wide = x.shape[1], x.shape[2]
    width = w_out.shape[1]
    slot = max(rows // n, 16)
    vmem = pl.BlockSpec(memory_space=pltpu.VMEM)
    bf16, f32 = jnp.bfloat16, jnp.float32
    dma = pltpu.SemaphoreType.DMA
    operands = (x, up, w_qkv, w_out, gain, bias, send_order, recv_order, lengths)
    operands = [pltpu.with_memory_space_constraint(a, pltpu.HBM) for a in operands]
    return pl.pallas_call(
        functools.partial(kernel, n, sections, sections % 2 == 0 and n <= 8),
        out_shape=jax.ShapeDtypeStruct(x.shape, bf16),
        in_specs=[pl.BlockSpec(memory_space=pltpu.HBM)] * 9,
        out_specs=vmem,
        scratch_shapes=[
            *[pltpu.VMEM(a.shape, a.dtype) for a in operands],
            dma((len(operands),)),
            pltpu.VMEM((n, slot, wide), bf16),
            pltpu.VMEM((n, slot, wide), bf16),
            pltpu.VMEM((n, slot, width), bf16),
            pltpu.VMEM((n, slot, width), bf16),
            pltpu.VMEM((n, slot, wide), bf16),
            pltpu.VMEM((n, slot, wide), bf16),
            pltpu.VMEM((rows, wide), bf16),
            pltpu.VMEM((8, rows), jnp.int32),
            pltpu.VMEM((8, rows), jnp.int32),
            pltpu.VMEM((rows, wide), f32),
            pltpu.VMEM((rows, width), bf16),
            pltpu.VMEM((rows, width), bf16),
            pltpu.VMEM((rows, width), bf16),
            pltpu.VMEM((width, rows), bf16),
            pltpu.VMEM((rows, width), bf16),
            pltpu.VMEM((rows, 128), bf16),
            pltpu.VMEM((rows, 128), bf16),
            pltpu.VMEM((width, rows), f32),
            pltpu.VMEM((width // HEAD * rows, rows), f32),
            pltpu.VMEM((rows, 3 * width), bf16),
            pltpu.VMEM((rows, 128), f32),
            pltpu.VMEM((rows, width), f32),
            pltpu.VMEM((rows, width), f32),
            dma((n,)),
            dma((n,)),
            dma((n,)),
            dma((n,)),
            dma((n,)),
            dma((n,)),
            dma((2,)),
            dma((2,)),
            pltpu.SemaphoreType.REGULAR,
        ],
        compiler_params=pltpu.CompilerParams(
            collective_id=0, has_side_effects=True, vmem_limit_bytes=40 * 1024 * 1024
        ),
        name="patch_attention_grad",
    )(*operands)


def solution(mesh):
    return jax.shard_map(
        per_device,
        mesh=mesh,
        in_specs=(
            P("section", "seq", None),
            P("section", "seq", None),
            P("section", None, None),
            P("section", None, None),
            P("section", None),
            P("section", None),
            P("section", "seq", None),
            P("section", "seq", None),
            P("section", "seq", None),
        ),
        out_specs=P("section", "seq", None),
        check_vma=False,
    )
```

```python
import functools
import math

import jax
import jax.numpy as jnp
from jax import lax
from jax.experimental import pallas as pl
from jax.experimental.pallas import tpu as pltpu
from jax.sharding import PartitionSpec as P

HEAD = 16
MESH = pl.DeviceIdType.MESH
LAST = (((1,), (1,)), ((), ()))
GROUP = 8


def dot(a, b):
    return jnp.dot(a, b, preferred_element_type=jnp.float32)


def dot_nt(a, b):
    return lax.dot_general(a, b, LAST, preferred_element_type=jnp.float32)


def each(first, count, body):
    if count - first <= 8:
        for step in by_distance(first, count):
            body(step)
    else:
        lax.fori_loop(first, count, lambda step, carry: (body(step), carry)[1], 0)


def by_distance(first, count):
    return sorted(range(first, count), key=lambda step: (abs(step - count // 2), step))


def iota(shape, axis):
    return lax.broadcasted_iota(jnp.int32, shape, axis)


def kernel(
    n,
    sections,
    paired,
    x_hbm,
    up_hbm,
    w_hbm,
    wo_hbm,
    gain_hbm,
    bias_hbm,
    send_hbm,
    recv_hbm,
    len_hbm,
    out_ref,
    x_ref,
    up_ref,
    w_ref,
    wo_ref,
    gain_ref,
    bias_ref,
    send_ref,
    recv_ref,
    len_ref,
    load_sem,
    send_x,
    recv_x,
    send_o,
    recv_o,
    send_b,
    recv_b,
    up_next,
    order_own,
    order_next,
    xhat_ref,
    q_ref,
    k_ref,
    v_ref,
    kt_ref,
    do_ref,
    feat_q,
    feat_k,
    dqt_ref,
    probs_ref,
    dqkv_ref,
    inverse_ref,
    dk_ref,
    dv_ref,
    sx_sem,
    rx_sem,
    so_sem,
    ro_sem,
    sb_sem,
    rb_sem,
    up_sem,
    order_sem,
    turn_sem,
):
    me = lax.axis_index("seq")
    section = lax.axis_index("section")
    rows, wide = x_ref.shape[1], x_ref.shape[2]
    width = wo_ref.shape[1]
    slot = send_x.shape[1]
    block = rows // n
    half = 128

    def spread(values):
        if slot == block:
            return values.reshape(n, slot, values.shape[1])
        place = iota((n * slot, rows), 0)
        source = jnp.where(place % slot < block, place // slot * block + place % slot, -1)
        pick = (source == iota((n * slot, rows), 1)).astype(jnp.bfloat16)
        return dot(pick, values).astype(jnp.bfloat16).reshape(n, slot, values.shape[1])

    def gather(values):
        values = values.reshape(n * slot, values.shape[2])
        if slot == block:
            return values
        place = iota((rows, n * slot), 0)
        pick = (place // block * slot + place % block == iota((rows, n * slot), 1)).astype(jnp.bfloat16)
        return dot(pick, values).astype(jnp.bfloat16)

    def x_copy(local, there, peer):
        return pltpu.make_async_remote_copy(
            send_x.at[local], recv_x.at[there], sx_sem.at[local], rx_sem.at[there],
            device_id=(peer, section), device_id_type=MESH,
        )

    def o_copy(local, there, peer):
        return pltpu.make_async_remote_copy(
            send_o.at[local], recv_o.at[there], so_sem.at[local], ro_sem.at[there],
            device_id=(peer, section), device_id_type=MESH,
        )

    def b_copy(local, there, peer):
        return pltpu.make_async_remote_copy(
            send_b.at[local], recv_b.at[there], sb_sem.at[local], rb_sem.at[there],
            device_id=(peer, section - 1), device_id_type=MESH,
        )

    def up_copy():
        return pltpu.make_async_remote_copy(
            up_ref.at[0], up_next, up_sem.at[0], up_sem.at[1],
            device_id=(me, section - 1), device_id_type=MESH,
        )

    def order_copy():
        return pltpu.make_async_remote_copy(
            order_own, order_next, order_sem.at[0], order_sem.at[1],
            device_id=(me, section - 1), device_id_type=MESH,
        )

    def x_sent(step):
        peer = lax.rem(me + step, n)
        x_copy(peer, me, peer).wait_send()

    far = by_distance(1, n)[:5] if paired else []
    loads = [
        pltpu.make_async_copy(source, target, load_sem.at[i])
        for i, (source, target) in enumerate(
            [
                (x_hbm, x_ref),
                (up_hbm, up_ref),
                (w_hbm, w_ref),
                (wo_hbm, wo_ref),
                (gain_hbm, gain_ref),
                (bias_hbm, bias_ref),
                (send_hbm, send_ref),
                (recv_hbm, recv_ref),
                (len_hbm, len_ref),
            ]
        )
    ]
    barrier = pltpu.get_barrier_semaphore()

    @pl.when(section > 0)
    def _():
        for i in (6, 0, 3, 1, 7, 8, 4, 5, 2):
            loads[i].start()

        def greet(step):
            pl.semaphore_signal(
                barrier, inc=1, device_id=(lax.rem(me + step, n), section), device_id_type=MESH
            )

        each(1, n, greet)

    @pl.when(section < sections - 1)
    def _():
        def greet(step):
            pl.semaphore_signal(
                barrier, inc=1, device_id=(lax.rem(me + step, n), section + 1), device_id_type=MESH
            )

        each(0, n, greet)

    first_of_pair = (section % 2 == 0) & (section > 0)
    second_of_pair = (section % 2 == 1) & (section > 1)
    if paired:

        @pl.when(second_of_pair)
        def _():
            pl.semaphore_signal(barrier, inc=1, device_id=(me, section - 1), device_id_type=MESH)

    @pl.when(section > 0)
    def _():
        loads[6].wait()
        order_own[...] = jnp.broadcast_to(send_ref[0], order_own.shape)
        row_of = send_ref[0].astype(jnp.float32)
        eye = iota((rows, rows), 0) == iota((rows, rows), 1)
        column = jnp.sum(jnp.where(eye, row_of, 0.0), axis=1, keepdims=True).astype(jnp.int32)
        pick = jnp.where(column == iota((rows, rows), 1), 1.0, 0.0).astype(jnp.bfloat16)
        loads[0].wait()
        send_x[...] = spread(dot(pick, x_ref[0]).astype(jnp.bfloat16))
        greetings = 2 * n - 1
        if paired:
            greetings = greetings + first_of_pair.astype(jnp.int32)
        pl.semaphore_wait(barrier, greetings)
        if paired:

            @pl.when(second_of_pair)
            def _():
                pl.semaphore_wait(turn_sem, 1)

        each(1, n, lambda step: x_copy(lax.rem(me + step, n), me, lax.rem(me + step, n)).start())
        loads[1].wait()
        loads[3].wait()
        out_common = dot_nt(up_ref[0], wo_ref[0]).astype(jnp.bfloat16)
        send_o[...] = spread(dot(pick, out_common).astype(jnp.bfloat16))
        each(1, n, lambda step: o_copy(lax.rem(me + step, n), me, lax.rem(me + step, n)).start())
        up_copy().start()
        order_copy().start()
        recv_x[me] = send_x[me]
        recv_o[me] = send_o[me]

        loads[7].wait()
        loads[8].wait()
        place = iota((1, rows), 1)
        end = jnp.zeros((1, 1), jnp.int32)
        segment = jnp.zeros((1, rows), jnp.float32)
        for patch in range(len_ref.shape[2]):
            end = end + len_ref[0, :, patch : patch + 1]
            segment = segment + jnp.where(place >= end, 1.0, 0.0)
        at = recv_ref[0] == iota((rows, rows), 0)
        patch_of = jnp.sum(jnp.where(at, segment, 0.0), axis=1, keepdims=True).astype(jnp.int32)
        lanes = iota((rows, half), 1)
        feat_k[...] = jnp.where(patch_of == lanes, 1.0, 0.0).astype(jnp.bfloat16)
        feat_q[...] = jnp.where(patch_of == lanes, 0.0, -1e30).astype(jnp.bfloat16)

        for i in (4, 5, 2):
            loads[i].wait()

        if paired:

            @pl.when(first_of_pair)
            def _():
                for step in far:
                    x_sent(step)
                pl.semaphore_signal(turn_sem, inc=1, device_id=(me, section + 1), device_id_type=MESH)

        pieces = 2 if slot == block and n % 2 == 0 else 1
        peers, few = n // pieces, rows // pieces
        for piece in range(pieces):
            which = lax.rem(me // peers + piece, pieces)
            some = pl.ds(pl.multiple_of(which * few, few), few)

            def x_wait(step, which=which):
                peer = which * peers + lax.rem(me + step, peers)
                x_copy(peer, peer, peer).wait_recv()

            each(1 if piece == 0 else 0, peers, x_wait)
            if pieces == 1:
                values = gather(recv_x[...])
            else:
                values = recv_x[pl.ds(which * peers, peers)].reshape(few, wide)
            values = values.astype(jnp.float32)
            centered = values - jnp.mean(values, axis=-1, keepdims=True)
            inverse = lax.rsqrt(jnp.mean(centered * centered, axis=-1, keepdims=True) + 1e-05)
            xhat = centered * inverse
            xhat_ref[some, :] = xhat
            inverse_ref[some, :] = jnp.broadcast_to(inverse, (few, half))
            normed = (xhat * gain_ref[...] + bias_ref[...]).astype(jnp.bfloat16)
            q_ref[some, :] = dot(normed, w_ref[0, :, :width]).astype(jnp.bfloat16)
            k_ref[some, :] = dot(normed, w_ref[0, :, width : 2 * width]).astype(jnp.bfloat16)
            v_ref[some, :] = dot(normed, w_ref[0, :, 2 * width :]).astype(jnp.bfloat16)
        kt_ref[...] = k_ref[...].astype(jnp.float32).T.astype(jnp.bfloat16)

        rate = float(HEAD) ** (-0.5) * math.log2(math.e)
        lane_head = iota((rows, half), 1) // HEAD
        zero = jnp.zeros((rows, half), jnp.bfloat16)
        groups = half // HEAD // GROUP

        def softmax_heads(part, group):
            columns = slice(part * half, (part + 1) * half)
            query_right = jnp.concatenate([q_ref[:, columns], feat_q[...]], axis=1)
            mine = [lane_head == group * GROUP + i for i in range(GROUP)]
            key, feature = k_ref[:, columns], feat_k[...]
            keys = jnp.concatenate(
                [jnp.concatenate([jnp.where(m, key, zero), feature], axis=1) for m in mine], axis=0
            )
            scores = dot_nt(keys, query_right)
            for i in range(GROUP):
                start = ((part * groups + group) * GROUP + i) * rows
                for first in range(0, rows, half):
                    some = slice(first, first + half)
                    score = scores[i * rows : (i + 1) * rows, some]
                    expo = jnp.exp2((score - jnp.max(score, axis=0, keepdims=True)) * rate)
                    probs_ref[pl.ds(start, rows), some] = expo * (1.0 / jnp.sum(expo, axis=0, keepdims=True))

        def gradient_heads(part, group):
            columns = slice(part * half, (part + 1) * half)
            query, value, dout = q_ref[:, columns], v_ref[:, columns], do_ref[:, columns]
            mine = [lane_head == group * GROUP + i for i in range(GROUP)]
            values = jnp.concatenate([jnp.where(m, value, zero) for m in mine], axis=0)
            dprobs = dot_nt(values, dout)
            weights, dscores = [], []
            for i in range(GROUP):
                start = ((part * groups + group) * GROUP + i) * rows
                weight, dscore = [], []
                for first in range(0, rows, half):
                    some = slice(first, first + half)
                    probs = probs_ref[pl.ds(start, rows), some]
                    dprob = dprobs[i * rows : (i + 1) * rows, some]
                    inner = jnp.sum(dprob * probs, axis=0, keepdims=True)
                    weight.append(probs.astype(jnp.bfloat16))
                    dscore.append((probs * (dprob - inner)).astype(jnp.bfloat16))
                weights.append(jnp.concatenate(weight, axis=1))
                dscores.append(jnp.concatenate(dscore, axis=1))
            dkeys = dot(jnp.concatenate(dscores, axis=0), query)
            dvalues = dot(jnp.concatenate(weights, axis=0), dout)
            dkey, dvalue = dk_ref[:, columns], dv_ref[:, columns]
            for i in range(GROUP):
                dkey = jnp.where(mine[i], dkeys[i * rows : (i + 1) * rows], dkey)
                dvalue = jnp.where(mine[i], dvalues[i * rows : (i + 1) * rows], dvalue)
                start = part * half + (group * GROUP + i) * HEAD
                dqt_ref[pl.ds(start, HEAD), :] = dot(kt_ref[pl.ds(start, HEAD), :], dscores[i])
            dk_ref[:, columns] = dkey
            dv_ref[:, columns] = dvalue

        def all_heads(some_heads):
            for part in range(width // half):
                for group in range(groups):
                    some_heads(part, group)

        all_heads(softmax_heads)

        def o_wait(step):
            peer = lax.rem(me + step, n)
            o_copy(peer, peer, peer).wait_recv()

        each(1, n, o_wait)
        do_ref[...] = gather(recv_o[...])
        all_heads(gradient_heads)

        scale = float(HEAD) ** (-0.5)
        dqkv_ref[:, :width] = (dqt_ref[...].T * scale).astype(jnp.bfloat16)
        dqkv_ref[:, width : 2 * width] = (dk_ref[...] * scale).astype(jnp.bfloat16)
        dqkv_ref[:, 2 * width :] = dv_ref[...].astype(jnp.bfloat16)
        for piece in range(pieces):
            which = lax.rem(me // peers + 1 + piece, pieces)
            some = pl.ds(pl.multiple_of(which * few, few), few)
            grad = dot_nt(dqkv_ref[some, :], w_ref[0]) * gain_ref[...]
            xhat = xhat_ref[some, :]
            mean = jnp.mean(grad, axis=-1, keepdims=True)
            cross = jnp.mean(grad * xhat, axis=-1, keepdims=True)
            branch = (inverse_ref[some, :1] * (grad - mean - xhat * cross)).astype(jnp.bfloat16)
            if pieces == 1:
                send_b[...] = spread(branch)
            else:
                send_b[pl.ds(which * peers, peers)] = branch.reshape(peers, slot, wide)

            def send_back(step, which=which):
                peer = which * peers + lax.rem(me + step, peers)
                b_copy(peer, me, peer).start()

            each(0, peers, send_back)

    @pl.when(section < sections - 1)
    def _():
        order_copy().wait_recv()
        up_copy().wait_recv()
        pick = jnp.where(order_next[0:1, :] == iota((rows, rows), 0), 1.0, 0.0).astype(jnp.bfloat16)

        def b_wait(step):
            peer = lax.rem(me + step, n)
            b_copy(peer, peer, peer).wait_recv()

        each(0, n, b_wait)
        branch = dot(pick, gather(recv_b[...]))
        out_ref[0] = (up_next[...].astype(jnp.float32) + branch).astype(jnp.bfloat16)

    @pl.when(section == sections - 1)
    def _():
        out_ref[...] = jnp.zeros_like(out_ref)

    @pl.when(section > 0)
    def _():
        def sent(step):
            peer = lax.rem(me + step, n)
            o_copy(peer, me, peer).wait_send()
            if not paired or step not in far:
                x_sent(step)
            else:

                @pl.when(jnp.logical_not(first_of_pair))
                def _():
                    x_sent(step)

        each(1, n, sent)

        def sent_back(step):
            peer = lax.rem(me + step, n)
            b_copy(peer, me, peer).wait_send()

        each(0, n, sent_back)
        up_copy().wait_send()
        order_copy().wait_send()


def per_device(x, up, w_qkv, w_out, gain, bias, send_order, recv_order, lengths):
    n, sections = lax.axis_size("seq"), lax.axis_size("section")
    rows, wide = x.shape[1], x.shape[2]
    width = w_out.shape[1]
    slot = max(rows // n, 16)
    vmem = pl.BlockSpec(memory_space=pltpu.VMEM)
    bf16, f32 = jnp.bfloat16, jnp.float32
    dma = pltpu.SemaphoreType.DMA
    operands = (x, up, w_qkv, w_out, gain, bias, send_order, recv_order, lengths)
    operands = [pltpu.with_memory_space_constraint(a, pltpu.HBM) for a in operands]
    return pl.pallas_call(
        functools.partial(kernel, n, sections, sections % 2 == 0 and n <= 8),
        out_shape=jax.ShapeDtypeStruct(x.shape, bf16),
        in_specs=[pl.BlockSpec(memory_space=pltpu.HBM)] * 9,
        out_specs=vmem,
        scratch_shapes=[
            *[pltpu.VMEM(a.shape, a.dtype) for a in operands],
            dma((len(operands),)),
            pltpu.VMEM((n, slot, wide), bf16),
            pltpu.VMEM((n, slot, wide), bf16),
            pltpu.VMEM((n, slot, width), bf16),
            pltpu.VMEM((n, slot, width), bf16),
            pltpu.VMEM((n, slot, wide), bf16),
            pltpu.VMEM((n, slot, wide), bf16),
            pltpu.VMEM((rows, wide), bf16),
            pltpu.VMEM((8, rows), jnp.int32),
            pltpu.VMEM((8, rows), jnp.int32),
            pltpu.VMEM((rows, wide), f32),
            pltpu.VMEM((rows, width), bf16),
            pltpu.VMEM((rows, width), bf16),
            pltpu.VMEM((rows, width), bf16),
            pltpu.VMEM((width, rows), bf16),
            pltpu.VMEM((rows, width), bf16),
            pltpu.VMEM((rows, 128), bf16),
            pltpu.VMEM((rows, 128), bf16),
            pltpu.VMEM((width, rows), f32),
            pltpu.VMEM((width // HEAD * rows, rows), f32),
            pltpu.VMEM((rows, 3 * width), bf16),
            pltpu.VMEM((rows, 128), f32),
            pltpu.VMEM((rows, width), f32),
            pltpu.VMEM((rows, width), f32),
            dma((n,)),
            dma((n,)),
            dma((n,)),
            dma((n,)),
            dma((n,)),
            dma((n,)),
            dma((2,)),
            dma((2,)),
            pltpu.SemaphoreType.REGULAR,
        ],
        compiler_params=pltpu.CompilerParams(
            collective_id=0, has_side_effects=True, vmem_limit_bytes=40 * 1024 * 1024
        ),
        name="patch_attention_grad",
    )(*operands)


def solution(mesh):
    return jax.shard_map(
        per_device,
        mesh=mesh,
        in_specs=(
            P("section", "seq", None),
            P("section", "seq", None),
            P("section", None, None),
            P("section", None, None),
            P("section", None),
            P("section", None),
            P("section", "seq", None),
            P("section", "seq", None),
            P("section", "seq", None),
        ),
        out_specs=P("section", "seq", None),
        check_vma=False,
    )
```
